32 devices in a mesh: dp: 16 (over z, y, core), space: 2 (over x).
Axes of the slice: x: 2, y: 2, z: 4, core: 2. Of those that a mesh axis runs over, the one named last changes fastest.
Arguments:
- fields: bfloat16 [16, 32, 16, 40, 128], P('dp', None, 'space'), may hold values from -6 to 6
- cotangent: bfloat16 [16, 32, 16, 40, 128], P('dp', None, 'space'), may hold values from -30 to 30
- spectral_weight: bfloat16 [16, 2, 32, 32, 144], P('space'), may hold values from -1 to 1
- channel_weight: bfloat16 [32, 32], replicated, may hold values from -1 to 1
- channel_bias: float32 [32], replicated, may hold values from -3 to 3
Outputs:
- grad_fields: bfloat16 [16, 32, 16, 40, 128], P('dp', None, 'space')
- grad_spectral: float32 [16, 2, 32, 32, 144], P('space')
- grad_channel: float32 [32, 32], replicated
- grad_bias: float32 [32], replicated
The draws below stay inside these ranges and needn't reach their ends.
All inputs are finite; a program needn't handle non-finite values.
Results may differ from the reference program's by a relative error of at most 0.02.
Values may be sent and summed in bfloat16 or wider, within the bound.
No kernel may reach another device: no remote copies, remote signals or barrier semaphores. Data moves between devices by JAX's collectives and lax.ppermute only.
A program may use at most 128 MiB of HBM per device.

```python
import math
import jax
import jax.numpy as jnp
from jax import lax

C = 32
MX = 16
MY = 16
MZ = 9
NY = 40
NZ = 128
NX = 16
BATCH = 16
P_SIZE = 144


def draw_cotangent(key, part):
    shape = (BATCH, C, NX, NY, NZ)
    cell_rise = jnp.arange(BATCH, dtype=jnp.float32) / max(BATCH - 1, 1)
    plane_rise = jnp.arange(NX, dtype=jnp.float32) / max(NX - 1, 1)
    factor = jnp.exp(math.log(3.0) * (cell_rise[:, None, None, None, None] + plane_rise[None, None, :, None, None]))
    base = jnp.clip(jax.random.normal(key, shape, jnp.float32), -6.0, 6.0)
    return (0.5 * base * factor).astype(jnp.bfloat16)


def block_scale(rng, extent, pieces, smallest, high):
    factor_of, own = 1.0, jax.random.fold_in(rng, 6)
    for dim, shards_of in pieces:
        steps = jnp.exp(jax.random.uniform(jax.random.fold_in(own, dim), (shards_of,), jnp.float32, smallest / len(pieces), high / len(pieces)))
        factor_of = factor_of * jnp.repeat(steps, extent[dim] // shards_of).reshape([-1 if axis == dim else 1 for axis in range(len(extent))])
    return factor_of


def bell_draw(rng, dims, width, reach, cuts=(), held_as=jnp.bfloat16):
    loudness = block_scale(rng, dims, cuts, -0.22, 0.18) if cuts else 1.0
    drawn = jax.random.normal(rng, dims, jnp.float32) * width * loudness
    return jnp.minimum(jnp.maximum(drawn, -reach), reach).astype(held_as)


def setup_inputs(seed: int = 0) -> dict:
    seeds = jax.random.split(jax.random.key(seed), 6)
    fields = bell_draw(seeds[0], (BATCH, C, NX, NY, NZ), 1.0, 6.0, ((0, 16), (2, 2)))
    cotangent = draw_cotangent(jax.random.fold_in(seeds[5], 71), 0)
    spectral_weight = bell_draw(seeds[2], (MX, 2, C, C, P_SIZE), C ** -0.5, 1.0, ((0, 2),))
    channel_weight = bell_draw(seeds[3], (C, C), C ** -0.5, 1.0)
    channel_bias = bell_draw(seeds[4], (C,), 0.5, 3.0, (), jnp.float32)
    return dict(fields=fields, cotangent=cotangent, spectral_weight=spectral_weight, channel_weight=channel_weight, channel_bias=channel_bias)


two_pi = 2.0 * math.pi
highest = lax.Precision.HIGHEST

def signed_index(index, modes):
    return jnp.where(index < modes // 2, index, index - modes)

def plane_table(ny_len, nz_len, my_modes, mz_modes):
    ky_modes = signed_index(jnp.arange(my_modes, dtype=jnp.int32), my_modes)
    kz_modes = jnp.arange(mz_modes, dtype=jnp.int32)
    y_pos = jnp.arange(ny_len, dtype=jnp.int32)
    z_pos = jnp.arange(nz_len, dtype=jnp.int32)
    phases = (y_pos[:, None, None, None] * ky_modes[None, None, :, None] * nz_len + z_pos[None, :, None, None] * kz_modes[None, None, None, :] * ny_len) % (ny_len * nz_len)
    angles = phases.astype(jnp.float32) * (two_pi / (ny_len * nz_len))
    row_count = ny_len * nz_len
    pair_count = my_modes * mz_modes
    cosine = jnp.cos(angles).reshape(row_count, pair_count)
    sines = -jnp.sin(angles).reshape(row_count, pair_count)
    return jnp.stack([cosine, sines], axis=1).astype(jnp.bfloat16)

def pair_weight(my_modes, mz_modes):
    kz_modes = jnp.arange(my_modes * mz_modes, dtype=jnp.int32) % mz_modes
    return jnp.where(kz_modes == 0, 1.0, 2.0).astype(jnp.float32)

def line_table(kx_index, x_pos, nx_len, mx_modes):
    kx_modes = signed_index(kx_index, mx_modes)
    phases = kx_modes[:, None] * x_pos[None, :] % nx_len
    angles = phases.astype(jnp.float32) * (two_pi / nx_len)
    cosine = jnp.cos(angles)
    sines = jnp.sin(angles)
    upper = jnp.stack([cosine, sines], axis=-1)
    lower = jnp.stack([-sines, cosine], axis=-1)
    return jnp.stack([upper, lower], axis=1)

def mix_modes(weights, spectrum):
    w_real, w_imag = (weights[:, 0], weights[:, 1])
    s_real, s_imag = (spectrum[:, :, :, 0], spectrum[:, :, :, 1])
    form = 'aiop,biap->boap'
    real = jnp.einsum(form, w_real, s_real, precision=highest) - jnp.einsum(form, w_imag, s_imag, precision=highest)
    imag = jnp.einsum(form, w_real, s_imag, precision=highest) + jnp.einsum(form, w_imag, s_real, precision=highest)
    return jnp.stack([real, imag], axis=3)

def mix_back(weights, grads):
    w_real, w_imag = (weights[:, 0], weights[:, 1])
    g_real, g_imag = (grads[:, :, :, 0], grads[:, :, :, 1])
    form = 'aiop,boap->biap'
    real = jnp.einsum(form, w_real, g_real, precision=highest) + jnp.einsum(form, w_imag, g_imag, precision=highest)
    imag = jnp.einsum(form, w_real, g_imag, precision=highest) - jnp.einsum(form, w_imag, g_real, precision=highest)
    return jnp.stack([real, imag], axis=3)

def weight_terms(spectrum, grads):
    s_real, s_imag = (spectrum[:, :, :, 0], spectrum[:, :, :, 1])
    g_real, g_imag = (grads[:, :, :, 0], grads[:, :, :, 1])
    form = 'boap,biap->aiop'
    real = jnp.einsum(form, g_real, s_real, precision=highest) + jnp.einsum(form, g_imag, s_imag, precision=highest)
    imag = jnp.einsum(form, g_imag, s_real, precision=highest) - jnp.einsum(form, g_real, s_imag, precision=highest)
    return jnp.stack([real, imag], axis=1)

def gelu_slope(values):
    return 0.5 * (1.0 + lax.erf(values * (1.0 / math.sqrt(2.0)))) + values * jnp.exp(-0.5 * values * values) * (1.0 / math.sqrt(2.0 * math.pi))

def rounded(values):
    return lax.optimization_barrier(values.astype(jnp.bfloat16)).astype(jnp.float32)

def reference(fields, cotangent, spectral_weight, channel_weight, channel_bias):
    scale = 1.0 / math.sqrt(NX * NY * NZ)
    basis = plane_table(NY, NZ, MY, MZ).astype(jnp.float32)
    kz_scale = pair_weight(MY, MZ)
    table = line_table(jnp.arange(MX, dtype=jnp.int32), jnp.arange(NX, dtype=jnp.int32), NX, MX)
    weights = spectral_weight.astype(jnp.float32)
    mixing = channel_weight.astype(jnp.float32)

    def one_cell(carry, inputs):
        cell, upstream = inputs
        flat = cell.reshape(1, C, NX, NY * NZ).astype(jnp.float32)
        plane_spec = rounded(jnp.einsum('bcxq,qjp->bcxjp', flat, basis))
        field_modes = scale * jnp.einsum('aixj,bcxjp->bcaip', table, plane_spec, precision=highest)
        mixed_modes = mix_modes(weights, field_modes)
        mixed_planes = rounded(jnp.einsum('aixj,bcaip->bcxjp', table, mixed_modes, precision=highest)) * kz_scale
        spectral_out = jnp.einsum('boxjp,qjp->boxq', mixed_planes, basis)
        local_out = jnp.einsum('oi,bixq->boxq', mixing, flat)
        summed = scale * spectral_out + local_out + channel_bias[None, :, None, None]
        upstream_flat = upstream.reshape(1, C, NX, NY * NZ).astype(jnp.float32)
        hidden = rounded(upstream_flat * gelu_slope(summed))
        back_planes = rounded(jnp.einsum('boxq,qjp->boxjp', hidden, basis) * (scale * kz_scale))
        grad_modes_out = jnp.einsum('aixj,bcxjp->bcaip', table, back_planes, precision=highest)
        grad_modes_in = mix_back(weights, grad_modes_out)
        grad_planes = rounded(scale * jnp.einsum('aixj,bcaip->bcxjp', table, grad_modes_in, precision=highest))
        spectral_back = jnp.einsum('bcxjp,qjp->bcxq', grad_planes, basis)
        local_back = jnp.einsum('oi,boxq->bixq', mixing, hidden)
        grad_cell = (spectral_back + local_back).astype(jnp.bfloat16).reshape(C, NX, NY, NZ)
        spectral_acc, channel_acc, bias_acc = carry
        spectral_acc = spectral_acc + weight_terms(field_modes, grad_modes_out)
        channel_acc = channel_acc + jnp.einsum('boxq,bixq->oi', hidden, flat)
        bias_acc = bias_acc + lax.optimization_barrier(jnp.sum(hidden, axis=(0, 2, 3)))
        return ((spectral_acc, channel_acc, bias_acc), grad_cell)
    start_carry = (jnp.zeros((MX, 2, C, C, MY * MZ), jnp.float32), jnp.zeros((C, C), jnp.float32), jnp.zeros((C,), jnp.float32))
    totals, grad_fields = lax.scan(one_cell, start_carry, (fields, cotangent))
    spectral_acc, channel_acc, bias_acc = totals
    cell_norm = 1.0 / math.sqrt(BATCH)
    voxel_norm = 1.0 / math.sqrt(BATCH * NX * NY * NZ)
    return (grad_fields, spectral_acc * cell_norm, channel_acc * voxel_norm, bias_acc * voxel_norm)
```

```python
import functools
import math

import jax
import jax.numpy as jnp
import ml_dtypes
import numpy as np
from jax import lax
from jax.experimental import pallas as pl
from jax.experimental.pallas import tpu as pltpu
from jax.sharding import PartitionSpec as P

MX = 16
MY = 16
MZ = 9
LANES = 128
BF16 = jnp.bfloat16
F32 = jnp.float32
VMEM_LIMIT = 50 * 1024 * 1024
TWO_PI = 2.0 * math.pi


def signed(index, modes):
    return np.where(index < modes // 2, index, index - modes)


def plane_columns(own):
    pairs = MY * MZ
    rest = pairs - LANES
    return np.concatenate([np.arange(LANES), LANES + np.tile(np.arange(rest), own)])


def plane_table(ny_len, nz_len, own):
    ky = signed(np.arange(MY), MY)
    kz = np.arange(MZ)
    y_pos = np.arange(ny_len)
    z_pos = np.arange(nz_len)
    phases = (
        y_pos[:, None, None, None] * ky[None, None, :, None] * nz_len
        + z_pos[None, :, None, None] * kz[None, None, None, :] * ny_len
    ) % (ny_len * nz_len)
    angles = phases.astype(np.float32) * np.float32(TWO_PI / (ny_len * nz_len))
    angles = angles.reshape(ny_len * nz_len, MY * MZ)
    columns = plane_columns(own)
    table = np.zeros((ny_len * nz_len, 2, 2 * LANES), np.float32)
    table[:, 0, : len(columns)] = np.cos(angles)[:, columns]
    table[:, 1, : len(columns)] = -np.sin(angles)[:, columns]
    return table.reshape(ny_len * nz_len, 4 * LANES).astype(ml_dtypes.bfloat16)


def column_weight(own, scale):
    columns = plane_columns(own)
    weight = np.zeros((2, 2 * LANES), np.float32)
    weight[:, : len(columns)] = np.where(columns % MZ == 0, 1.0, 2.0)
    return (weight * scale).reshape(1, 4 * LANES).astype(np.float32)


def line_tables(chans, planes, count):
    own = MX // count
    length = planes * count
    tables = []
    for s in range(count):
        place = (s + np.arange(count)) % count
        index = (place[:, None] * own + np.arange(own)[None, :]).reshape(-1)
        phases = signed(index, MX)[:, None] * (s * planes + np.arange(planes))[None, :] % length
        angles = phases.astype(np.float32) * np.float32(TWO_PI / length)
        cosine, sines = np.cos(angles), np.sin(angles)
        line = np.stack([np.stack([cosine, sines], -1), np.stack([-sines, cosine], -1)], 1)
        whole = np.einsum("arxj,cd->arcjdx", line, np.eye(chans, dtype=np.float32))
        tables.append(whole.reshape(MX * 2 * chans, 2 * chans * planes))
    return np.stack(tables).astype(ml_dtypes.bfloat16)


def dot(left, right):
    return jnp.dot(left, right, preferred_element_type=F32)


def dot_nt(left, right):
    return lax.dot_general(left, right, (((1,), (1,)), ((), ())), preferred_element_type=F32)


def tail_mask(a, rows, rest):
    lane = lax.broadcasted_iota(jnp.int32, (rows, LANES), 1)
    return (lane >= a * rest) & (lane < (a + 1) * rest)


def spread_rows(block_ref, rows_ref, out_ref, start):
    count, ny_len, nz_len = block_ref.shape
    rows_ref[...] = block_ref[...].astype(F32).reshape(count * ny_len, nz_len)
    for y in range(ny_len):
        piece = rows_ref[pl.ds(y, count, stride=ny_len), :]
        out_ref[pl.ds(start, count), y * nz_len : (y + 1) * nz_len] = piece.astype(BF16)


def emit_modes(terms, refs, own, rest):
    height = terms.shape[0] // (own * len(refs))
    for k, ref in enumerate(refs):
        tail = jnp.zeros((height, LANES), F32)
        for a in range(own):
            first = (k * own + a) * height
            block = terms[first : first + height]
            ref[a] = block[:, :LANES].astype(ref.dtype)
            tail = jnp.where(tail_mask(a, height, rest), block[:, LANES:], tail)
        ref[own] = tail.astype(ref.dtype)


def line_forward(spec, line_ref):
    half = 2 * LANES
    depth = line_ref.shape[2] // 2
    return dot(line_ref[0, :, :depth], spec[:, :half]) + dot(line_ref[0, :, depth:], spec[:, half:])


def planes_of(mode_refs, inverse_ref, weight_ref, stack_ref, planes_ref, own, rest):
    height = mode_refs[0].shape[1]
    half = 2 * LANES
    for k, ref in enumerate(mode_refs):
        tail = ref[own].astype(F32)
        for a in range(own):
            first = (k * own + a) * height
            stack_ref[first : first + height, :LANES] = ref[a]
            masked = jnp.where(tail_mask(a, height, rest), tail, 0.0)
            stack_ref[first : first + height, LANES:] = masked.astype(BF16)
    depth = inverse_ref.shape[1] // 2
    for j in range(2):
        part = dot(inverse_ref[0, j * depth : (j + 1) * depth, :], stack_ref[...])
        columns = slice(j * half, (j + 1) * half)
        planes_ref[:, columns] = (part * weight_ref[:, columns]).astype(BF16)


def gelu_slope(values):
    size = jnp.abs(values) * (1.0 / math.sqrt(2.0))
    bell = jnp.exp(-(size * size))
    t = 1.0 / (1.0 + 0.3275911 * size)
    poly = t * (
        0.127414796 + t * (-0.142248368 + t * (0.7107068705 + t * (-0.7265760135 + t * 0.5307027145)))
    )
    tail = poly * bell
    upper = jnp.where(values >= 0.0, 1.0 - tail, tail)
    return upper + values * bell * (1.0 / math.sqrt(2.0 * math.pi))


def forward_kernel(own, rest, count, s_ref, fields_ref, line_ref, basis_hbm, flat_ref, *more):
    outs, (rows_ref, basis_ref, sem) = more[:count], more[count:]
    step = pl.program_id(0)
    copy = pltpu.make_async_copy(basis_hbm, basis_ref, sem)

    @pl.when(step == 0)
    def _():
        copy.start()

    rows = fields_ref.shape[0]
    spread_rows(fields_ref, rows_ref, flat_ref, pl.multiple_of(step * rows, rows))

    @pl.when(step == pl.num_programs(0) - 1)
    def _():
        copy.wait()
        spec = dot(flat_ref[...], basis_ref[...]).astype(BF16)
        emit_modes(line_forward(spec, line_ref), outs, own, rest)


def relayout_kernel(block_ref, out_ref, rows_ref):
    spread_rows(block_ref, rows_ref, out_ref, 0)


def sum_modes(mode_refs, scale, total_ref, out_ref, own):
    for blk in range(own + 1):
        total = mode_refs[0][blk]
        for ref in mode_refs[1:]:
            total = total + ref[blk].astype(F32)
        total = total * scale
        total_ref[blk] = total
        out_ref[blk] = total.astype(BF16)


def load_wide(total_ref, wide_ref, a, own, rest):
    wide_ref[:, :LANES] = total_ref[a]
    wide_ref[:, LANES:] = pltpu.roll(total_ref[own], lax.rem(LANES - a * rest, LANES), 1)


def store_wide(wide_ref, tail_ref, out_ref, a, own, rest):
    out_ref[a] = wide_ref[:, :LANES].astype(BF16)
    moved = pltpu.roll(wide_ref[:, LANES:], a * rest, 1)
    height = moved.shape[0]
    tail_ref[...] = jnp.where(tail_mask(a, height, rest), moved, tail_ref[...])

    @pl.when(a == own - 1)
    def _():
        out_ref[own] = tail_ref[...].astype(BF16)


def mix_kernel(own, rest, count, scale, *refs):
    modes, (weight_ref, out_ref, sum_ref) = refs[:count], refs[count : count + 3]
    total_ref, wide_ref, result_ref, tail_ref = refs[count + 3 :]
    a = pl.program_id(0)

    @pl.when(a == 0)
    def _():
        sum_modes(modes, scale, total_ref, sum_ref, own)
        result_ref[...] = jnp.zeros_like(result_ref)
        tail_ref[...] = jnp.zeros_like(tail_ref)

    load_wide(total_ref, wide_ref, a, own, rest)
    chans = weight_ref.shape[2]
    pairs = weight_ref.shape[4]
    real = jnp.zeros((chans, pairs), F32)
    imag = jnp.zeros((chans, pairs), F32)
    for i in range(chans):
        w_real = weight_ref[0, 0, i].astype(F32)
        w_imag = weight_ref[0, 1, i].astype(F32)
        u_real = wide_ref[i : i + 1, :pairs]
        u_imag = wide_ref[chans + i : chans + i + 1, :pairs]
        real = real + (w_real * u_real - w_imag * u_imag)
        imag = imag + (w_real * u_imag + w_imag * u_real)
    result_ref[:chans, :pairs] = real
    result_ref[chans:, :pairs] = imag
    store_wide(result_ref, tail_ref, out_ref, a, own, rest)


def mix_back_kernel(own, rest, count, *refs):
    modes, (chan_ref, weight_ref, out_ref, sum_ref) = refs[:count], refs[count : count + 4]
    total_ref, wide_ref, result_ref, tail_ref = refs[count + 4 :]
    a = pl.program_id(0)
    chans = weight_ref.shape[2]
    pairs = weight_ref.shape[4]

    @pl.when(a == 0)
    def _():
        sum_modes(modes, 1.0, total_ref, sum_ref, own)
        chan = chan_ref[...]
        for ref in modes[1:]:
            chan = chan + (ref[own + 1, :chans].astype(F32) + ref[own + 1, chans:].astype(F32))
        upper = chan.astype(BF16)
        sum_ref[own + 1, :chans] = upper
        sum_ref[own + 1, chans:] = (chan - upper.astype(F32)).astype(BF16)
        result_ref[...] = jnp.zeros_like(result_ref)
        tail_ref[...] = jnp.zeros_like(tail_ref)

    load_wide(total_ref, wide_ref, a, own, rest)
    g_real = wide_ref[:chans, :pairs]
    g_imag = wide_ref[chans:, :pairs]
    for i in range(chans):
        w_real = weight_ref[0, 0, i].astype(F32)
        w_imag = weight_ref[0, 1, i].astype(F32)
        real = jnp.sum(w_real * g_real + w_imag * g_imag, axis=0, keepdims=True)
        imag = jnp.sum(w_real * g_imag - w_imag * g_real, axis=0, keepdims=True)
        result_ref[i : i + 1, :pairs] = real
        result_ref[chans + i : chans + i + 1, :pairs] = imag
    store_wide(result_ref, tail_ref, out_ref, a, own, rest)


def middle_kernel(own, rest, count, planes, s_ref, *refs):
    modes, refs = refs[:count], refs[count:]
    inverse_ref, line_ref, weight_ref, mix_ref, bias_ref, flat_ref, cot_ref, basis_ref = refs[:8]
    hidden_ref, chan_ref, refs = refs[8], refs[9], refs[10:]
    outs, (stack_ref, planes_ref, back_ref, cross_ref) = refs[:count], refs[count:]
    step = pl.program_id(0)

    @pl.when(step == 0)
    def _():
        planes_of(modes, inverse_ref, weight_ref, stack_ref, planes_ref, own, rest)
        back_ref[...] = jnp.zeros_like(back_ref)
        cross_ref[...] = jnp.zeros_like(cross_ref)

    flat = flat_ref[...]
    summed = dot_nt(planes_ref[...], basis_ref[...]) + dot(mix_ref[...], flat) + bias_ref[...]
    hidden = (cot_ref[...].astype(F32) * gelu_slope(summed)).astype(BF16)
    hidden_ref[...] = hidden
    back_ref[...] += dot(hidden, basis_ref[...])
    cross_ref[...] += dot_nt(hidden, flat)

    @pl.when(step == pl.num_programs(0) - 1)
    def _():
        back = back_ref[...]
        spec = (back * weight_ref[...]).astype(BF16)
        emit_modes(line_forward(spec, line_ref), outs, own, rest)
        rows = cross_ref.shape[0]
        chans = rows // planes
        row = lax.broadcasted_iota(jnp.int32, (rows, rows), 0)
        column = lax.broadcasted_iota(jnp.int32, (rows, rows), 1)
        same = lax.rem(row, planes) == lax.rem(column, planes)
        cross = jnp.where(same, cross_ref[...], 0.0)
        row = lax.broadcasted_iota(jnp.int32, (chans, rows), 0)
        column = lax.broadcasted_iota(jnp.int32, (chans, rows), 1)
        group = jnp.where((column >= row * planes) & (column < (row + 1) * planes), 1.0, 0.0)
        row = lax.broadcasted_iota(jnp.int32, (rows, LANES), 0)
        column = lax.broadcasted_iota(jnp.int32, (rows, LANES), 1)
        place = jnp.where((row >= column * planes) & (row < (column + 1) * planes), 1.0, 0.0)
        exact = functools.partial(jnp.dot, preferred_element_type=F32, precision=lax.Precision.HIGHEST)
        sums = jnp.where(column == chans, back[:, :1], 0.0)
        chan = exact(group, exact(cross, place) + sums)
        chan_ref[...] = chan
        upper = chan.astype(BF16)
        lower = (chan - upper.astype(F32)).astype(BF16)
        for ref in outs[1:]:
            ref[own + 1, :chans] = upper
            ref[own + 1, chans:] = lower


def last_kernel(own, rest, count, steps, s_ref, *refs):
    modes, refs = refs[:count], refs[count:]
    inverse_ref, weight_ref, mix_ref, hidden_ref, basis_ref, out_ref = refs[:6]
    stack_ref, planes_ref, rows_ref = refs[6:]
    step = pl.program_id(0)
    block, ny_len, nz_len = out_ref.shape
    rows = planes_ref.shape[0]

    @pl.when(step == 0)
    def _():
        planes_of(modes, inverse_ref, weight_ref, stack_ref, planes_ref, own, rest)

    @pl.when(step < steps)
    def _():
        total = dot_nt(planes_ref[...], basis_ref[...]) + dot(mix_ref[...], hidden_ref[...])
        group = total.shape[1] // nz_len
        for y in range(group):
            rows_ref[pl.ds(step * group + y, rows, stride=ny_len), :] = total[:, y * nz_len : (y + 1) * nz_len]

    @pl.when(step >= steps)
    def _():
        start = pl.multiple_of((step - steps) * (block * ny_len), block * ny_len)
        piece = rows_ref[pl.ds(start, block * ny_len), :]
        out_ref[...] = piece.reshape(block, ny_len, nz_len).astype(BF16)


def outer_kernel(own, rest, cells, cell_norm, voxel_norm, *refs):
    u_refs, g_refs, c_refs = refs[:cells], refs[cells : 2 * cells], refs[2 * cells : 3 * cells]
    out_ref, chan_ref, u_all, g_all, tail_ref = refs[3 * cells :]
    step = pl.program_id(0)
    chans = g_all.shape[2]
    for b in range(cells):
        g_real = g_refs[b][0, :chans].astype(F32)
        g_imag = g_refs[b][0, chans:].astype(F32)
        u_real = u_refs[b][0, :chans].astype(F32) * cell_norm
        u_imag = u_refs[b][0, chans:].astype(F32) * cell_norm
        g_all[b, 0] = g_real + g_imag
        g_all[b, 1] = g_real
        g_all[b, 2] = g_imag
        u_all[b, 0] = u_real
        u_all[b, 1] = u_real + u_imag
        u_all[b, 2] = u_real - u_imag

    def products(i):
        sums = [None] * 3
        for b in range(cells):
            for t in range(3):
                term = u_all[b, t, pl.ds(i, 1), :] * g_all[b, t]
                sums[t] = term if sums[t] is None else sums[t] + term
        return sums[0] - sums[2], sums[0] - sums[1]

    @pl.when(step == 0)
    def _():
        chan = jnp.zeros(chan_ref.shape, F32)
        for ref in c_refs:
            chan = chan + (ref[0, :chans].astype(F32) + ref[0, chans:].astype(F32))
        chan_ref[...] = chan * voxel_norm

        @pl.loop(0, chans)
        def _(i):
            real, imag = products(i)
            tail_ref[0, i] = real
            tail_ref[1, i] = imag

    @pl.when(step > 0)
    def _():
        a = step - 1
        shift = lax.rem(LANES - a * rest, LANES)

        @pl.loop(0, chans)
        def _(i):
            for r, main in enumerate(products(i)):
                out_ref[0, r, i, :, :LANES] = main
                moved = pltpu.roll(tail_ref[r, i], shift, 1)
                out_ref[0, r, i, :, LANES:] = moved[:, :rest]


def params(**kw):
    return pltpu.CompilerParams(vmem_limit_bytes=VMEM_LIMIT, **kw)


def whole(shape):
    return pl.BlockSpec(shape, lambda *_: (0,) * len(shape))


def at_place(shape):
    return pl.BlockSpec((1,) + shape, lambda i, s: (s[0],) + (0,) * len(shape))


def relayout(array, rows):
    total, ny_len, nz_len = array.shape
    return pl.pallas_call(
        relayout_kernel,
        grid=(total // rows,),
        in_specs=[pl.BlockSpec((rows, ny_len, nz_len), lambda i: (i, 0, 0))],
        out_specs=pl.BlockSpec((rows, ny_len * nz_len), lambda i: (i, 0)),
        out_shape=jax.ShapeDtypeStruct((total, ny_len * nz_len), BF16),
        scratch_shapes=[pltpu.VMEM((rows * ny_len, nz_len), F32)],
        compiler_params=params(),
        name="relayout",
    )(array)


def send(array, axis, count, shift):
    return lax.ppermute(array, axis, [(i, (i + shift) % count) for i in range(count)])


def swap(array, bit, count):
    return lax.ppermute(array, "dp", [(i, i ^ bit) for i in range(count)])


def gather_cells(array, count):
    if count & (count - 1) or count < 4:
        every = lax.all_gather(array, "dp")
        return [every[b] for b in range(count)]
    pieces = [array, swap(array, 2, count)]
    for z in range(1, count // 4):
        far = swap(array, 4 * z, count)
        pieces += [far, swap(far, 2, count)]
    return pieces + [swap(piece, 1, count) for piece in pieces]


def shards(count, cell_count, fields, cotangent, spectral_weight, channel_weight, channel_bias):
    _, chans, planes, ny_len, nz_len = fields.shape
    own, _, _, _, pairs = spectral_weight.shape
    rest = pairs - LANES
    rows = chans * planes
    columns = ny_len * nz_len
    block = min(rows, 64)
    scale = 1.0 / math.sqrt(planes * count * columns)
    cell_norm = 1.0 / math.sqrt(cell_count)
    voxel_norm = 1.0 / math.sqrt(cell_count * planes * count * columns)
    height = 2 * chans
    wide = 4 * LANES

    basis = jnp.asarray(plane_table(ny_len, nz_len, own))
    line_np = line_tables(chans, planes, count)
    line = jnp.asarray(line_np)
    inverse = jnp.asarray(np.ascontiguousarray(np.swapaxes(line_np, 1, 2)))
    up_weight = jnp.asarray(column_weight(own, scale))
    down_weight = jnp.full((1, wide), scale, F32)
    place = lax.axis_index("space").astype(jnp.int32).reshape(1)
    eye = jnp.eye(planes, dtype=BF16)
    mix_up = jnp.einsum("oi,xw->oxiw", channel_weight, eye).reshape(rows, rows)
    mix_down = jnp.einsum("oi,xw->ixow", channel_weight, eye).reshape(rows, rows)
    bias = jnp.repeat(channel_bias, planes).reshape(rows, 1)

    modes = jax.ShapeDtypeStruct((own + 1, height, LANES), F32)
    sent = jax.ShapeDtypeStruct((own + 1, height, LANES), BF16)
    tagged = jax.ShapeDtypeStruct((own + 2, height, LANES), BF16)

    flat, mine, *others = pl.pallas_call(
        functools.partial(forward_kernel, own, rest, count),
        grid_spec=pltpu.PrefetchScalarGridSpec(
            num_scalar_prefetch=1,
            grid=(rows // block,),
            in_specs=[
                pl.BlockSpec((block, ny_len, nz_len), lambda i, s: (i, 0, 0)),
                at_place(line.shape[1:]),
                pl.BlockSpec(memory_space=pl.ANY),
            ],
            out_specs=[whole((rows, columns)), whole(modes.shape)] + [whole(sent.shape)] * (count - 1),
            scratch_shapes=[
                pltpu.VMEM((block * ny_len, nz_len), F32),
                pltpu.VMEM(basis.shape, BF16),
                pltpu.SemaphoreType.DMA,
            ],
        ),
        out_shape=[jax.ShapeDtypeStruct((rows, columns), BF16), modes] + [sent] * (count - 1),
        compiler_params=params(),
        name="forward",
    )(place, fields.reshape(rows, ny_len, nz_len), line, basis)
    cot = relayout(cotangent.reshape(rows, ny_len, nz_len), block)
    arrived = [send(array, "space", count, k + 1) for k, array in enumerate(others)]

    weight_spec = pl.BlockSpec((1,) + spectral_weight.shape[1:], lambda a: (a, 0, 0, 0, 0))
    mix_scratch = [
        pltpu.VMEM(modes.shape, F32),
        pltpu.VMEM((height, 2 * LANES), F32),
        pltpu.VMEM((height, 2 * LANES), F32),
        pltpu.VMEM((height, LANES), F32),
    ]
    mixed, field_modes = pl.pallas_call(
        functools.partial(mix_kernel, own, rest, count, scale),
        grid=(own,),
        in_specs=[whole(modes.shape)] * count + [weight_spec],
        out_specs=[whole(sent.shape), whole(sent.shape)],
        out_shape=[sent, sent],
        scratch_shapes=mix_scratch,
        compiler_params=params(),
        name="mix",
    )(mine, *arrived, spectral_weight)

    all_mixed = [mixed] + [send(mixed, "space", count, -k) for k in range(1, count)]
    all_u = gather_cells(field_modes, cell_count)
    step_columns = 4 * nz_len
    steps = columns // step_columns
    hidden, chan, mine, *others = pl.pallas_call(
        functools.partial(middle_kernel, own, rest, count, planes),
        grid_spec=pltpu.PrefetchScalarGridSpec(
            num_scalar_prefetch=1,
            grid=(steps,),
            in_specs=[whole(sent.shape)] * count
            + [
                at_place(inverse.shape[1:]),
                at_place(line.shape[1:]),
                whole((1, wide)),
                whole((rows, rows)),
                whole((rows, 1)),
                pl.BlockSpec((rows, step_columns), lambda i, s: (0, i)),
                pl.BlockSpec((rows, step_columns), lambda i, s: (0, i)),
                pl.BlockSpec((step_columns, wide), lambda i, s: (i, 0)),
            ],
            out_specs=[
                pl.BlockSpec((rows, step_columns), lambda i, s: (0, i)),
                whole((chans, LANES)),
                whole(modes.shape),
            ]
            + [whole(tagged.shape)] * (count - 1),
            scratch_shapes=[
                pltpu.VMEM((count * own * height, 2 * LANES), BF16),
                pltpu.VMEM((rows, wide), BF16),
                pltpu.VMEM((rows, wide), F32),
                pltpu.VMEM((rows, rows), F32),
            ],
        ),
        out_shape=[
            jax.ShapeDtypeStruct((rows, columns), BF16),
            jax.ShapeDtypeStruct((chans, LANES), F32),
            modes,
        ]
        + [tagged] * (count - 1),
        compiler_params=params(),
        name="middle",
    )(place, *all_mixed, inverse, line, up_weight, mix_up, bias, flat, cot, basis)
    arrived = [send(array, "space", count, k + 1) for k, array in enumerate(others)]

    returned, grad_modes = pl.pallas_call(
        functools.partial(mix_back_kernel, own, rest, count),
        grid=(own,),
        in_specs=[whole(modes.shape)] + [whole(tagged.shape)] * (count - 1) + [whole((chans, LANES)), weight_spec],
        out_specs=[whole(sent.shape), whole(tagged.shape)],
        out_shape=[sent, tagged],
        scratch_shapes=mix_scratch,
        compiler_params=params(),
        name="mix_back",
    )(mine, *arrived, chan, spectral_weight)

    all_g = gather_cells(grad_modes, cell_count)
    all_returned = [returned] + [send(returned, "space", count, -k) for k in range(1, count)]
    grad_fields = pl.pallas_call(
        functools.partial(last_kernel, own, rest, count, steps),
        grid_spec=pltpu.PrefetchScalarGridSpec(
            num_scalar_prefetch=1,
            grid=(steps + rows // block,),
            in_specs=[whole(sent.shape)] * count
            + [
                at_place(inverse.shape[1:]),
                whole((1, wide)),
                whole((rows, rows)),
                pl.BlockSpec((rows, step_columns), lambda i, s: (0, jnp.minimum(i, steps - 1))),
                pl.BlockSpec((step_columns, wide), lambda i, s: (jnp.minimum(i, steps - 1), 0)),
            ],
            out_specs=pl.BlockSpec((block, ny_len, nz_len), lambda i, s: (jnp.maximum(i - steps, 0), 0, 0)),
            scratch_shapes=[
                pltpu.VMEM((count * own * height, 2 * LANES), BF16),
                pltpu.VMEM((rows, wide), BF16),
                pltpu.VMEM((rows * ny_len, nz_len), F32),
            ],
        ),
        out_shape=jax.ShapeDtypeStruct((rows, ny_len, nz_len), BF16),
        compiler_params=params(),
        name="last",
    )(place, *all_returned, inverse, down_weight, mix_down, hidden, basis)

    one = pl.BlockSpec((1, height, LANES), lambda i: (jnp.where(i == 0, own, i - 1), 0, 0))
    tag = pl.BlockSpec((1, height, LANES), lambda i: (own + 1, 0, 0))
    grad_spectral, chan_total = pl.pallas_call(
        functools.partial(outer_kernel, own, rest, cell_count, cell_norm, voxel_norm),
        grid=(own + 1,),
        in_specs=[one] * (2 * cell_count) + [tag] * cell_count,
        out_specs=[
            pl.BlockSpec((1,) + spectral_weight.shape[1:], lambda i: (jnp.maximum(i - 1, 0), 0, 0, 0, 0)),
            whole((chans, LANES)),
        ],
        out_shape=[
            jax.ShapeDtypeStruct(spectral_weight.shape, F32),
            jax.ShapeDtypeStruct((chans, LANES), F32),
        ],
        scratch_shapes=[
            pltpu.VMEM((cell_count, 3, chans, LANES), F32),
            pltpu.VMEM((cell_count, 3, chans, LANES), F32),
            pltpu.VMEM((2, chans, chans, LANES), F32),
        ],
        compiler_params=params(),
        name="outer",
    )(*all_u, *all_g, *all_g)
    return (grad_fields.reshape(fields.shape), grad_spectral, chan_total[:, :chans], chan_total[:, chans])


def solution(mesh):
    in_specs = (
        P("dp", None, "space", None, None),
        P("dp", None, "space", None, None),
        P("space", None, None, None, None),
        P(),
        P(),
    )
    out_specs = (P("dp", None, "space", None, None), P("space", None, None, None, None), P(), P())
    body = functools.partial(shards, mesh.shape["space"], mesh.shape["dp"])
    return jax.shard_map(body, mesh=mesh, in_specs=in_specs, out_specs=out_specs, check_vma=False)
```

```python
import functools
import math

import jax
import jax.numpy as jnp
import ml_dtypes
import numpy as np
from jax import lax
from jax.experimental import pallas as pl
from jax.experimental.pallas import tpu as pltpu
from jax.sharding import PartitionSpec as P

MX = 16
MY = 16
MZ = 9
LANES = 128
BF16 = jnp.bfloat16
F32 = jnp.float32
TWO_PI = 2.0 * math.pi


def signed(index, modes):
    return np.where(index < modes // 2, index, index - modes)


def plane_columns(own):
    pairs = MY * MZ
    rest = pairs - LANES
    return np.concatenate([np.arange(LANES), LANES + np.tile(np.arange(rest), own)])


def plane_table(ny_len, nz_len, own):
    ky = signed(np.arange(MY), MY)
    kz = np.arange(MZ)
    y_pos = np.arange(ny_len)
    z_pos = np.arange(nz_len)
    phases = (
        y_pos[:, None, None, None] * ky[None, None, :, None] * nz_len
        + z_pos[None, :, None, None] * kz[None, None, None, :] * ny_len
    ) % (ny_len * nz_len)
    angles = phases.astype(np.float32) * np.float32(TWO_PI / (ny_len * nz_len))
    angles = angles.reshape(ny_len * nz_len, MY * MZ)
    columns = plane_columns(own)
    table = np.zeros((ny_len * nz_len, 2, 2 * LANES), np.float32)
    table[:, 0, : len(columns)] = np.cos(angles)[:, columns]
    table[:, 1, : len(columns)] = -np.sin(angles)[:, columns]
    return table.reshape(ny_len * nz_len, 4 * LANES).astype(ml_dtypes.bfloat16)


def column_weight(own, scale):
    columns = plane_columns(own)
    weight = np.zeros((2, 2 * LANES), np.float32)
    weight[:, : len(columns)] = np.where(columns % MZ == 0, 1.0, 2.0)
    return (weight * scale).reshape(1, 4 * LANES).astype(np.float32)


def line_tables(chans, planes, count):
    own = MX // count
    length = planes * count
    tables = []
    for s in range(count):
        place = (s + np.arange(count)) % count
        index = (place[:, None] * own + np.arange(own)[None, :]).reshape(-1)
        phases = signed(index, MX)[:, None] * (s * planes + np.arange(planes))[None, :] % length
        angles = phases.astype(np.float32) * np.float32(TWO_PI / length)
        cosine, sines = np.cos(angles), np.sin(angles)
        line = np.stack([np.stack([cosine, sines], -1), np.stack([-sines, cosine], -1)], 1)
        whole = np.einsum("arxj,cd->arcjdx", line, np.eye(chans, dtype=np.float32))
        tables.append(whole.reshape(MX * 2 * chans, 2 * chans * planes))
    return np.stack(tables).astype(ml_dtypes.bfloat16)


def dot(left, right):
    return jnp.dot(left, right, preferred_element_type=F32)


def dot_nt(left, right):
    return lax.dot_general(left, right, (((1,), (1,)), ((), ())), preferred_element_type=F32)


def tail_mask(a, rows, rest):
    lane = lax.broadcasted_iota(jnp.int32, (rows, LANES), 1)
    return (lane >= a * rest) & (lane < (a + 1) * rest)


def spread_rows(block_ref, out_ref, start, count):
    _, ny_len, nz_len = block_ref.shape
    turned = jnp.swapaxes(block_ref[start : start + count], 0, 1)
    for y in range(ny_len):
        out_ref[start : start + count, y * nz_len : (y + 1) * nz_len] = turned[y]


def emit_modes(terms, refs, own, rest):
    height = terms.shape[0] // (own * len(refs))
    for k, ref in enumerate(refs):
        tail = jnp.zeros((height, LANES), F32)
        for a in range(own):
            first = (k * own + a) * height
            block = terms[first : first + height]
            ref[a] = block[:, :LANES].astype(ref.dtype)
            tail = jnp.where(tail_mask(a, height, rest), block[:, LANES:], tail)
        ref[own] = tail.astype(ref.dtype)


def line_forward(spec, line):
    half = 2 * LANES
    depth = line.shape[1] // 2
    return dot(line[:, :depth], spec[:, :half]) + dot(line[:, depth:], spec[:, half:])


def planes_of(mode_refs, inverse, weight_ref, stack_ref, planes_ref, own, rest):
    height = mode_refs[0].shape[1]
    half = 2 * LANES
    for k, ref in enumerate(mode_refs):
        tail = ref[own].astype(F32)
        for a in range(own):
            first = (k * own + a) * height
            stack_ref[first : first + height, :LANES] = ref[a]
            masked = jnp.where(tail_mask(a, height, rest), tail, 0.0)
            stack_ref[first : first + height, LANES:] = masked.astype(BF16)
    depth = inverse.shape[0] // 2
    for j in range(2):
        part = dot(inverse[j * depth : (j + 1) * depth, :], stack_ref[...])
        columns = slice(j * half, (j + 1) * half)
        planes_ref[:, columns] = (part * weight_ref[:, columns]).astype(BF16)


def gelu_slope(values):
    bell = jnp.exp(-0.5 * values * values) * (1.0 / math.sqrt(2.0 * math.pi))
    return 0.5 * (1.0 + lax.erf(values * (1.0 / math.sqrt(2.0)))) + values * bell


def iota(shape, axis):
    return lax.broadcasted_iota(jnp.int32, shape, axis)


def forward_kernel(own, rest, count, s_ref, fields_hbm, basis_hbm, line_hbm, flat_ref, *refs):
    outs, refs = refs[:count], refs[count:]
    fields_ref, basis_ref, line_ref, fields_sem, basis_sem, line_sem = refs
    rows, _, _ = fields_ref.shape
    parts = fields_sem.shape[0]
    part = rows // parts
    pieces = basis_sem.shape[0]
    piece = basis_ref.shape[0] // pieces
    fields = [
        pltpu.make_async_copy(
            fields_hbm.at[pl.ds(k * part, part)], fields_ref.at[pl.ds(k * part, part)], fields_sem.at[k]
        )
        for k in range(parts)
    ]
    basis = [
        pltpu.make_async_copy(
            basis_hbm.at[pl.ds(k * piece, piece)], basis_ref.at[pl.ds(k * piece, piece)], basis_sem.at[k]
        )
        for k in range(pieces)
    ]
    line = pltpu.make_async_copy(line_hbm.at[s_ref[0]], line_ref, line_sem)
    for copy in fields + basis + [line]:
        copy.start()
    for k, copy in enumerate(fields):
        copy.wait()
        spread_rows(fields_ref, flat_ref, k * part, part)
    total = None
    for k, copy in enumerate(basis):
        copy.wait()
        span = slice(k * piece, (k + 1) * piece)
        term = dot(flat_ref[:, span], basis_ref[span])
        total = term if total is None else total + term
    line.wait()
    emit_modes(line_forward(total.astype(BF16), line_ref[...]), outs, own, rest)


def prepare_kernel(planes, part, cot_hbm, weight_hbm, flat_ref, channel_ref, bias_ref, *refs):
    out_ref, local_ref, down_ref, weight_ref, cot_ref, sem = refs
    cot_copy = pltpu.make_async_copy(cot_hbm, cot_ref, sem.at[0])
    cot_copy.start()
    weight_copy = pltpu.make_async_copy(weight_hbm, weight_ref, sem.at[1])
    weight_copy.start()
    rows, columns = flat_ref.shape
    chans = rows // planes
    row = iota((rows, chans), 0)
    column = iota((rows, chans), 1)
    member = (row >= column * planes) & (row < (column + 1) * planes)
    spread = jnp.where(member, 1.0, 0.0).astype(BF16)
    same = lax.rem(iota((rows, rows), 0), planes) == lax.rem(iota((rows, rows), 1), planes)
    channel = channel_ref[...]
    up = dot_nt(dot(spread, channel).astype(BF16), spread)
    down = dot_nt(dot_nt(spread, channel).astype(BF16), spread)
    up = jnp.where(same, up, 0.0).astype(BF16)
    down_ref[...] = jnp.where(same, down, 0.0).astype(BF16)
    bias = jnp.sum(jnp.where(member, bias_ref[...], 0.0), axis=1, keepdims=True)
    step = 8 * LANES
    for k in range(columns // step):
        span = slice(k * step, (k + 1) * step)
        local_ref[:, span] = dot(up, flat_ref[:, span]) + bias
    cot_copy.wait()
    for k in range(rows // part):
        spread_rows(cot_ref, out_ref, k * part, part)
    weight_copy.wait()


def sum_modes(mode_refs, scale, total_ref, out_ref, own):
    for blk in range(own + 1):
        total = mode_refs[0][blk]
        for ref in mode_refs[1:]:
            total = total + ref[blk].astype(F32)
        total = total * scale
        total_ref[blk] = total
        out_ref[blk] = total.astype(BF16)


def load_wide(total_ref, wide_ref, a, own, rest):
    wide_ref[:, :LANES] = total_ref[a]
    wide_ref[:, LANES:] = pltpu.roll(total_ref[own], lax.rem(LANES - a * rest, LANES), 1)


def store_wide(wide_ref, tail_ref, out_ref, a, own, rest):
    out_ref[a] = wide_ref[:, :LANES].astype(BF16)
    moved = pltpu.roll(wide_ref[:, LANES:], a * rest, 1)
    height = moved.shape[0]
    tail_ref[...] = jnp.where(tail_mask(a, height, rest), moved, tail_ref[...])

    @pl.when(a == own - 1)
    def _():
        out_ref[own] = tail_ref[...].astype(BF16)


def mix_kernel(own, rest, count, scale, *refs):
    refs = refs[1:]
    modes, (weight_ref, out_ref, sum_ref) = refs[:count], refs[count : count + 3]
    total_ref, wide_ref, result_ref, tail_ref = refs[count + 3 :]
    chans = weight_ref.shape[2]
    pairs = weight_ref.shape[4]
    sum_modes(modes, scale, total_ref, sum_ref, own)
    result_ref[...] = jnp.zeros_like(result_ref)
    tail_ref[...] = jnp.zeros_like(tail_ref)

    @pl.loop(0, own)
    def _(a):
        load_wide(total_ref, wide_ref, a, own, rest)
        real = jnp.zeros((chans, pairs), F32)
        imag = jnp.zeros((chans, pairs), F32)
        for i in range(chans):
            w_real = weight_ref[a, 0, i].astype(F32)
            w_imag = weight_ref[a, 1, i].astype(F32)
            u_real = wide_ref[i : i + 1, :pairs]
            u_imag = wide_ref[chans + i : chans + i + 1, :pairs]
            real = real + (w_real * u_real - w_imag * u_imag)
            imag = imag + (w_real * u_imag + w_imag * u_real)
        result_ref[:chans, :pairs] = real
        result_ref[chans:, :pairs] = imag
        store_wide(result_ref, tail_ref, out_ref, a, own, rest)


def total_kernel(own, count, *refs):
    modes, (chan_ref, total_ref, sum_ref) = refs[:count], refs[count:]
    chans = chan_ref.shape[0]
    sum_modes(modes, 1.0, total_ref, sum_ref, own)
    chan = chan_ref[...]
    for ref in modes[1:]:
        chan = chan + (ref[own + 1, :chans].astype(F32) + ref[own + 1, chans:].astype(F32))
    upper = chan.astype(BF16)
    sum_ref[own + 1, :chans] = upper
    sum_ref[own + 1, chans:] = (chan - upper.astype(F32)).astype(BF16)


def mix_back_kernel(own, rest, ties, *refs):
    total_ref, weight_ref, out_ref, wide_ref, result_ref, tail_ref, part_ref = refs[ties:]
    chans = weight_ref.shape[2]
    pairs = weight_ref.shape[4]
    group = 8
    result_ref[...] = jnp.zeros_like(result_ref)
    tail_ref[...] = jnp.zeros_like(tail_ref)

    @pl.loop(0, own)
    def _(a):
        load_wide(total_ref, wide_ref, a, own, rest)
        g_real = wide_ref[:chans, :pairs]
        g_imag = wide_ref[chans:, :pairs]
        for i in range(chans):
            w_real = weight_ref[a, 0, i].astype(F32)
            w_imag = weight_ref[a, 1, i].astype(F32)
            real = w_real * g_real + w_imag * g_imag
            imag = w_real * g_imag - w_imag * g_real
            real = sum(real[k : k + group] for k in range(0, chans, group))
            imag = sum(imag[k : k + group] for k in range(0, chans, group))
            for r, value in enumerate((real, imag)):
                first = (r * chans + i) * group
                part_ref[0, first : first + group, :] = value[:, :LANES]
                part_ref[1, first : first + group, : pairs - LANES] = value[:, LANES:]
        for half in range(2):
            rows = [part_ref[half, pl.ds(k, 2 * chans, stride=group), :] for k in range(group)]
            result_ref[:, half * LANES : (half + 1) * LANES] = sum(rows[1:], rows[0])
        store_wide(result_ref, tail_ref, out_ref, a, own, rest)


def middle_kernel(own, rest, count, planes, ties, s_ref, *refs):
    refs = refs[ties:]
    modes, refs = refs[:count], refs[count:]
    inverse_ref, line_ref, weight_ref, flat_ref, cot_ref, local_ref, basis_ref = refs[:7]
    hidden_ref, chan_ref, refs = refs[7], refs[8], refs[9:]
    outs, (stack_ref, planes_ref) = refs[:count], refs[count:]
    planes_of(modes, inverse_ref[s_ref[0]], weight_ref, stack_ref, planes_ref, own, rest)
    rows, columns = flat_ref.shape
    step = 4 * LANES
    back = jnp.zeros((rows, weight_ref.shape[1]), F32)
    cross = jnp.zeros((rows, rows), F32)
    for k in range(columns // step):
        span = slice(k * step, (k + 1) * step)
        summed = dot_nt(planes_ref[...], basis_ref[span]) + local_ref[:, span]
        hidden = (cot_ref[:, span].astype(F32) * gelu_slope(summed)).astype(BF16)
        hidden_ref[:, span] = hidden
        back = back + dot(hidden, basis_ref[span])
        cross = cross + dot_nt(hidden, flat_ref[:, span])
    spec = (back * weight_ref[...]).astype(BF16)
    emit_modes(line_forward(spec, line_ref[s_ref[0]]), outs, own, rest)
    chans = rows // planes
    same = lax.rem(iota((rows, rows), 0), planes) == lax.rem(iota((rows, rows), 1), planes)
    cross = jnp.where(same, cross, 0.0)
    row, column = iota((chans, rows), 0), iota((chans, rows), 1)
    group = jnp.where((column >= row * planes) & (column < (row + 1) * planes), 1.0, 0.0)
    row, column = iota((rows, LANES), 0), iota((rows, LANES), 1)
    place = jnp.where((row >= column * planes) & (row < (column + 1) * planes), 1.0, 0.0)
    exact = functools.partial(jnp.dot, preferred_element_type=F32, precision=lax.Precision.HIGHEST)
    sums = jnp.where(column == chans, back[:, :1], 0.0)
    chan = exact(group, exact(cross, place) + sums)
    chan_ref[...] = chan
    upper = chan.astype(BF16)
    lower = (chan - upper.astype(F32)).astype(BF16)
    for ref in outs[1:]:
        ref[own + 1, :chans] = upper
        ref[own + 1, chans:] = lower


def last_kernel(own, rest, count, part, ties, s_ref, *refs):
    refs = refs[ties:]
    modes, refs = refs[:count], refs[count:]
    inverse_ref, weight_ref, mix_ref, hidden_ref, basis_ref, out_hbm = refs[:6]
    stack_ref, planes_ref, turned_ref, out_ref, sem = refs[6:]
    rows, ny_len, nz_len = out_ref.shape
    planes_of(modes, inverse_ref[s_ref[0]], weight_ref, stack_ref, planes_ref, own, rest)
    group = 4
    step = group * nz_len
    for k in range(ny_len // group):
        span = slice(k * step, (k + 1) * step)
        total = dot_nt(planes_ref[...], basis_ref[span]) + dot(mix_ref[...], hidden_ref[:, span])
        total = total.astype(BF16)
        for y in range(group):
            turned_ref[k * group + y] = total[:, y * nz_len : (y + 1) * nz_len]
    copies = []
    for k in range(rows // part):
        span = slice(k * part, (k + 1) * part)
        out_ref[span] = jnp.swapaxes(turned_ref[:, span], 0, 1)
        here = pl.ds(k * part, part)
        copies.append(pltpu.make_async_copy(out_ref.at[here], out_hbm.at[here], sem.at[k]))
        copies[-1].start()
    for copy in copies:
        copy.wait()


def load_cells(u_refs, g_refs, u_all, g_all, factor):
    chans = g_all.shape[2]
    for b, (u_ref, g_ref) in enumerate(zip(u_refs, g_refs, strict=True)):
        g_real = g_ref[0, :chans].astype(F32)
        g_imag = g_ref[0, chans:].astype(F32)
        u_real = u_ref[0, :chans].astype(F32) * factor
        u_imag = u_ref[0, chans:].astype(F32) * factor
        g_all[b, 0] = g_real + g_imag
        g_all[b, 1] = g_real
        g_all[b, 2] = g_imag
        u_all[b, 0] = u_real
        u_all[b, 1] = u_real + u_imag
        u_all[b, 2] = u_real - u_imag


TOGETHER = 4


def products(u_all, g_all, first):
    sums = [[None] * 3 for _ in range(TOGETHER)]
    for b in range(u_all.shape[0]):
        for t in range(3):
            grad = g_all[b, t]
            for k in range(TOGETHER):
                term = u_all[b, t, pl.ds(first + k, 1), :] * grad
                sums[k][t] = term if sums[k][t] is None else sums[k][t] + term
    return [(part[0] - part[2], part[0] - part[1]) for part in sums]


def tag_sum(refs, chans):
    total = jnp.zeros((chans, LANES), F32)
    for ref in refs:
        total = total + (ref[0, :chans].astype(F32) + ref[0, chans:].astype(F32))
    return total


def early_kernel(cells, ties, factor, *refs):
    refs = refs[ties:]
    u_refs, g_refs, c_refs = refs[:cells], refs[cells : 2 * cells], refs[2 * cells : 3 * cells]
    out_ref, chan_ref, u_all, g_all = refs[3 * cells :]
    chans = g_all.shape[2]
    load_cells(u_refs, g_refs, u_all, g_all, factor)

    @pl.when(pl.program_id(0) == 0)
    def _():
        chan_ref[...] = tag_sum(c_refs, chans)

    @pl.loop(0, chans, step=TOGETHER)
    def _(i):
        for k, parts in enumerate(products(u_all, g_all, i)):
            for r, part in enumerate(parts):
                out_ref[0, r, i + k] = part.astype(BF16)


def outer_kernel(rest, cells, sums, factor, norm, *refs):
    u_refs, g_refs, c_refs = refs[:cells], refs[cells : 2 * cells], refs[2 * cells : 3 * cells]
    refs = refs[3 * cells :]
    sum_refs, sum_chans, refs = refs[:sums], refs[sums : 2 * sums], refs[2 * sums :]
    out_ref, chan_ref, bias_ref, u_all, g_all, tail_ref = refs
    step = pl.program_id(0)
    chans = g_all.shape[2]
    load_cells(u_refs, g_refs, u_all, g_all, factor)

    def totals(i):
        for k, parts in enumerate(products(u_all, g_all, i)):
            for r, part in enumerate(parts):
                for ref in sum_refs:
                    part = part + ref[0, r, i + k].astype(F32)
                yield r, i + k, part

    @pl.when(step == 0)
    def _():
        chan = tag_sum(c_refs, chans)
        for ref in sum_chans:
            chan = chan + ref[...]
        chan = chan * norm
        chan_ref[...] = chan[:, :chans]
        same = iota((chans, LANES), 0) == iota((chans, LANES), 1)
        bias = jnp.sum(jnp.where(same, chan[:, chans : chans + 1], 0.0), axis=0, keepdims=True)
        bias_ref[...] = bias[:, :chans]

        @pl.loop(0, chans, step=TOGETHER)
        def _(i):
            for r, at, part in totals(i):
                tail_ref[r, at] = part

    @pl.when(step > 0)
    def _():
        shift = lax.rem(LANES - (step - 1) * rest, LANES)

        @pl.loop(0, chans, step=TOGETHER)
        def _(i):
            for r, at, part in totals(i):
                out_ref[0, r, at, :, :LANES] = part
                out_ref[0, r, at, :, LANES:] = pltpu.roll(tail_ref[r, at], shift, 1)[:, :rest]


def about(microseconds):
    return pl.CostEstimate(
        flops=int(microseconds * 1.15e9), bytes_accessed=int(microseconds * 3.6e6), transcendentals=0
    )


def call(kernel, name, time, ins, outs, scratch=(), limit=16):
    return pl.pallas_call(
        kernel,
        in_specs=ins,
        out_specs=[pl.BlockSpec(memory_space=out[2] if len(out) > 2 else pltpu.VMEM) for out in outs],
        out_shape=[jax.ShapeDtypeStruct(*out[:2]) for out in outs],
        scratch_shapes=list(scratch),
        compiler_params=pltpu.CompilerParams(vmem_limit_bytes=limit * 1024 * 1024),
        cost_estimate=about(time),
        name=name,
    )


def here(number):
    return [pl.BlockSpec(memory_space=pltpu.VMEM)] * number


def there(number):
    return [pl.BlockSpec(memory_space=pltpu.HBM)] * number


def send(array, axis, count, shift):
    return lax.ppermute(array, axis, [(i, (i + shift) % count) for i in range(count)])


def swap(array, bit, count):
    return lax.ppermute(array, "dp", [(i, i ^ bit) for i in range(count)])


def first_cells(array, count):
    if count & (count - 1) or count < 8:
        return []
    return [array, swap(array, 2, count)] + [swap(array, 4 * z, count) for z in range(1, count // 4)]


def order_cells(array, first, count):
    if not first:
        return [], list(lax.all_gather(array, "dp"))
    near = first[:2] + [piece for far in first[2:] for piece in (far, swap(far, 2, count))]
    return near[: len(near) // 2], near[len(near) // 2 :]


def scratch_cells(cells, chans):
    return [pltpu.VMEM((cells, 3, chans, LANES), F32)] * 2


def early_gradient(all_u, all_g, ties, own, cell_norm):
    cells = len(all_u)
    chans = all_u[0].shape[1] // 2
    block = (1,) + all_u[0].shape[1:]
    one = pl.BlockSpec(block, lambda i: (i, 0, 0))
    tag = pl.BlockSpec(block, lambda i: (own + 1, 0, 0))
    return pl.pallas_call(
        functools.partial(early_kernel, cells, len(ties), cell_norm),
        grid=(own + 1,),
        in_specs=there(len(ties)) + [one] * (2 * cells) + [tag] * cells,
        out_specs=[
            pl.BlockSpec((1, 2, chans, chans, LANES), lambda i: (i, 0, 0, 0, 0)),
            pl.BlockSpec((chans, LANES), lambda i: (0, 0)),
        ],
        out_shape=[
            jax.ShapeDtypeStruct((own + 1, 2, chans, chans, LANES), BF16),
            jax.ShapeDtypeStruct((chans, LANES), F32),
        ],
        scratch_shapes=scratch_cells(cells, chans),
        compiler_params=pltpu.CompilerParams(vmem_limit_bytes=16 * 1024 * 1024),
        cost_estimate=about(4.8),
        name="early",
    )(*ties, *all_u, *all_g, *all_g)


def weight_gradient(all_u, all_g, sums, weight_shape, norms):
    own, _, chans, _, pairs = weight_shape
    cell_norm, voxel_norm = norms
    block = (1,) + all_u[0].shape[1:]
    cells = len(all_u)
    at = lambda i: jnp.where(i == 0, own, i - 1)
    one = pl.BlockSpec(block, lambda i: (at(i), 0, 0))
    tag = pl.BlockSpec(block, lambda i: (own + 1, 0, 0))
    add = pl.BlockSpec((1, 2, chans, chans, LANES), lambda i: (at(i), 0, 0, 0, 0))
    add_chan = pl.BlockSpec((chans, LANES), lambda i: (0, 0))
    half = len(sums) // 2
    return pl.pallas_call(
        functools.partial(outer_kernel, pairs - LANES, cells, half, cell_norm, voxel_norm),
        grid=(own + 1,),
        in_specs=[one] * (2 * cells) + [tag] * cells + [add] * half + [add_chan] * half,
        out_specs=[
            pl.BlockSpec((1,) + weight_shape[1:], lambda i: (jnp.maximum(i - 1, 0), 0, 0, 0, 0)),
            pl.BlockSpec((chans, chans), lambda i: (0, 0)),
            pl.BlockSpec((1, chans), lambda i: (0, 0)),
        ],
        out_shape=[
            jax.ShapeDtypeStruct(weight_shape, F32),
            jax.ShapeDtypeStruct((chans, chans), F32),
            jax.ShapeDtypeStruct((1, chans), F32),
        ],
        scratch_shapes=scratch_cells(cells, chans) + [pltpu.VMEM((2, chans, chans, LANES), F32)],
        compiler_params=pltpu.CompilerParams(vmem_limit_bytes=20 * 1024 * 1024),
        cost_estimate=about(12.8),
        name="outer",
    )(*all_u, *all_g, *all_g, *sums)


def shards(count, cell_count, fields, cotangent, spectral_weight, channel_weight, channel_bias):
    _, chans, planes, ny_len, nz_len = fields.shape
    own, _, _, _, pairs = spectral_weight.shape
    rest = pairs - LANES
    rows = chans * planes
    columns = ny_len * nz_len
    block = min(rows, 64)
    scale = 1.0 / math.sqrt(planes * count * columns)
    cell_norm = 1.0 / math.sqrt(cell_count)
    voxel_norm = 1.0 / math.sqrt(cell_count * planes * count * columns)
    height = 2 * chans
    wide = 4 * LANES

    basis = jnp.asarray(plane_table(ny_len, nz_len, own))
    line_np = line_tables(chans, planes, count)
    line = jnp.asarray(line_np)
    inverse = jnp.asarray(np.ascontiguousarray(np.swapaxes(line_np, 1, 2)))
    up_weight = jnp.asarray(column_weight(own, scale))
    down_weight = jnp.asarray(np.full((1, wide), scale, np.float32))
    place = lax.axis_index("space").astype(jnp.int32).reshape(1)

    modes = ((own + 1, height, LANES), F32)
    sent = ((own + 1, height, LANES), BF16)
    tagged = ((own + 2, height, LANES), BF16)
    grid_like = (rows, ny_len, nz_len)

    flat, mine, *others = call(
        functools.partial(forward_kernel, own, rest, count),
        "forward",
        4.3,
        [pl.BlockSpec(memory_space=pltpu.SMEM)] + there(3),
        [((rows, columns), BF16), modes] + [sent] * (count - 1),
        [
            pltpu.VMEM(grid_like, BF16),
            pltpu.VMEM(basis.shape, BF16),
            pltpu.VMEM(line.shape[1:], BF16),
            pltpu.SemaphoreType.DMA((rows // block,)),
            pltpu.SemaphoreType.DMA((5,)),
            pltpu.SemaphoreType.DMA,
        ],
        52,
    )(place, fields.reshape(grid_like), basis, line)
    arrived = [send(array, "space", count, k + 1) for k, array in enumerate(others)]
    cot, local, mix_down, weights = call(
        functools.partial(prepare_kernel, planes, block),
        "prepare",
        2.5,
        there(2) + here(3),
        [((rows, columns), BF16), ((rows, columns), F32), ((rows, rows), BF16), (spectral_weight.shape, BF16)],
        [pltpu.VMEM(grid_like, BF16), pltpu.SemaphoreType.DMA((2,))],
        28,
    )(cotangent.reshape(grid_like), spectral_weight, flat, channel_weight, channel_bias.reshape(1, chans))

    mix_scratch = [
        pltpu.VMEM((height, 2 * LANES), F32),
        pltpu.VMEM((height, 2 * LANES), F32),
        pltpu.VMEM((height, LANES), F32),
    ]
    mixed, field_modes = call(
        functools.partial(mix_kernel, own, rest, count, scale),
        "mix",
        3.9,
        there(1) + here(count + 1),
        [sent, sent],
        [pltpu.VMEM(modes[0], F32)] + mix_scratch,
    )(cot, mine, *arrived, weights)

    u_first = first_cells(field_modes, cell_count)
    ties = u_first[1:3]
    all_mixed = [mixed] + [send(mixed, "space", count, -k) for k in range(1, count)]
    plane_scratch = [pltpu.VMEM((count * own * height, 2 * LANES), BF16), pltpu.VMEM((rows, wide), BF16)]
    hidden, chan, mine, *others = call(
        functools.partial(middle_kernel, own, rest, count, planes, len(ties)),
        "middle",
        6.3,
        [pl.BlockSpec(memory_space=pltpu.SMEM)] + there(len(ties)) + here(count + 7),
        [((rows, columns), BF16), ((chans, LANES), F32), modes] + [tagged] * (count - 1),
        plane_scratch,
    )(place, *ties, *all_mixed, inverse, line, up_weight, flat, cot, local, basis)
    arrived = [send(array, "space", count, k + 1) for k, array in enumerate(others)]

    total, grad_modes = call(
        functools.partial(total_kernel, own, count), "total", 1.0, here(count + 1), [modes, tagged]
    )(mine, *arrived, chan)
    ties = u_first[3:]
    (returned,) = call(
        functools.partial(mix_back_kernel, own, rest, len(ties)),
        "mix_back",
        4.1,
        there(len(ties)) + here(2),
        [sent],
        mix_scratch + [pltpu.VMEM((2, 2 * chans * 8, LANES), F32)],
    )(*ties, total, weights)

    g_first = first_cells(grad_modes, cell_count)
    all_returned = [returned] + [send(returned, "space", count, -k) for k in range(1, count)]
    early_u, late_u = order_cells(field_modes, u_first, cell_count)
    early_g, late_g = order_cells(grad_modes, g_first, cell_count)
    sums = []
    if early_u:
        late_u = late_u + [swap(piece, 1, cell_count) for piece in late_u]
        ties = all_returned + g_first[3:] + late_u
        part, part_chan = early_gradient(early_u, early_g, ties, own, cell_norm)
        sums = [part, swap(part, 1, cell_count), part_chan, swap(part_chan, 1, cell_count)]
        late_g = late_g + [swap(piece, 1, cell_count) for piece in late_g]
    ties = sums[:1]
    (grad_fields,) = call(
        functools.partial(last_kernel, own, rest, count, block, len(ties)),
        "last",
        4.4,
        [pl.BlockSpec(memory_space=pltpu.SMEM)] + there(len(ties)) + here(count + 5),
        [(grid_like, BF16, pltpu.HBM)],
        plane_scratch
        + [
            pltpu.VMEM((ny_len, rows, nz_len), BF16),
            pltpu.VMEM(grid_like, BF16),
            pltpu.SemaphoreType.DMA((rows // block,)),
        ],
    )(place, *ties, *all_returned, inverse, down_weight, mix_down, hidden, basis)

    grad_spectral, grad_channel, grad_bias = weight_gradient(
        late_u, late_g, sums, spectral_weight.shape, (cell_norm, voxel_norm)
    )
    return (grad_fields.reshape(fields.shape), grad_spectral, grad_channel, grad_bias.reshape(chans))


def solution(mesh):
    in_specs = (
        P("dp", None, "space", None, None),
        P("dp", None, "space", None, None),
        P("space", None, None, None, None),
        P(),
        P(),
    )
    out_specs = (P("dp", None, "space", None, None), P("space", None, None, None, None), P(), P())
    body = functools.partial(shards, mesh.shape["space"], mesh.shape["dp"])
    return jax.shard_map(body, mesh=mesh, in_specs=in_specs, out_specs=out_specs, check_vma=False)
```

```python
import functools
import math

import jax
import jax.numpy as jnp
import ml_dtypes
import numpy as np
from jax import lax
from jax.experimental import pallas as pl
from jax.experimental.pallas import tpu as pltpu
from jax.sharding import PartitionSpec as P

MX = 16
MY = 16
MZ = 9
LANES = 128
BF16 = jnp.bfloat16
F32 = jnp.float32
TWO_PI = 2.0 * math.pi


def signed(index, modes):
    return np.where(index < modes // 2, index, index - modes)


def plane_columns(own):
    pairs = MY * MZ
    rest = pairs - LANES
    return np.concatenate([np.arange(LANES), LANES + np.tile(np.arange(rest), own)])


def plane_table(ny_len, nz_len, own):
    ky = signed(np.arange(MY), MY)
    kz = np.arange(MZ)
    y_pos = np.arange(ny_len)
    z_pos = np.arange(nz_len)
    phases = (
        y_pos[:, None, None, None] * ky[None, None, :, None] * nz_len
        + z_pos[None, :, None, None] * kz[None, None, None, :] * ny_len
    ) % (ny_len * nz_len)
    angles = phases.astype(np.float32) * np.float32(TWO_PI / (ny_len * nz_len))
    angles = angles.reshape(ny_len * nz_len, MY * MZ)
    columns = plane_columns(own)
    table = np.zeros((ny_len * nz_len, 2, 2 * LANES), np.float32)
    table[:, 0, : len(columns)] = np.cos(angles)[:, columns]
    table[:, 1, : len(columns)] = -np.sin(angles)[:, columns]
    return table.reshape(ny_len * nz_len, 4 * LANES).astype(ml_dtypes.bfloat16)


def column_weight(own, scale):
    columns = plane_columns(own)
    weight = np.zeros((2, 2 * LANES), np.float32)
    weight[:, : len(columns)] = np.where(columns % MZ == 0, 1.0, 2.0)
    return (weight * scale).reshape(1, 4 * LANES).astype(np.float32)


def line_tables(chans, planes, count):
    own = MX // count
    length = planes * count
    tables = []
    for s in range(count):
        place = (s + np.arange(count)) % count
        index = (place[:, None] * own + np.arange(own)[None, :]).reshape(-1)
        phases = signed(index, MX)[:, None] * (s * planes + np.arange(planes))[None, :] % length
        angles = phases.astype(np.float32) * np.float32(TWO_PI / length)
        cosine, sines = np.cos(angles), np.sin(angles)
        line = np.stack([np.stack([cosine, sines], -1), np.stack([-sines, cosine], -1)], 1)
        whole = np.einsum("arxj,cd->arcjdx", line, np.eye(chans, dtype=np.float32))
        tables.append(whole.reshape(MX * 2 * chans, 2 * chans * planes))
    return np.stack(tables).astype(ml_dtypes.bfloat16)


def dot(left, right):
    return jnp.dot(left, right, preferred_element_type=F32)


def dot_nt(left, right):
    return lax.dot_general(left, right, (((1,), (1,)), ((), ())), preferred_element_type=F32)


def tail_mask(a, rows, rest):
    lane = lax.broadcasted_iota(jnp.int32, (rows, LANES), 1)
    return (lane >= a * rest) & (lane < (a + 1) * rest)


def spread_rows(block_ref, out_ref, start, count):
    _, ny_len, nz_len = block_ref.shape
    turned = jnp.swapaxes(block_ref[start : start + count], 0, 1)
    for y in range(ny_len):
        out_ref[start : start + count, y * nz_len : (y + 1) * nz_len] = turned[y]


def emit_modes(terms, refs, own, rest):
    height = terms.shape[0] // (own * len(refs))
    for k, ref in enumerate(refs):
        tail = jnp.zeros((height, LANES), F32)
        for a in range(own):
            first = (k * own + a) * height
            block = terms[first : first + height]
            ref[a] = block[:, :LANES].astype(ref.dtype)
            tail = jnp.where(tail_mask(a, height, rest), block[:, LANES:], tail)
        ref[own] = tail.astype(ref.dtype)


def line_forward(spec, line):
    half = 2 * LANES
    depth = line.shape[1] // 2
    return dot(line[:, :depth], spec[:, :half]) + dot(line[:, depth:], spec[:, half:])


def planes_of(mode_refs, inverse, weight_ref, stack_ref, planes_ref, own, rest):
    height = mode_refs[0].shape[1]
    half = 2 * LANES
    for k, ref in enumerate(mode_refs):
        tail = ref[own].astype(F32)
        for a in range(own):
            first = (k * own + a) * height
            stack_ref[first : first + height, :LANES] = ref[a]
            masked = jnp.where(tail_mask(a, height, rest), tail, 0.0)
            stack_ref[first : first + height, LANES:] = masked.astype(BF16)
    depth = inverse.shape[0] // 2
    for j in range(2):
        part = dot(inverse[j * depth : (j + 1) * depth, :], stack_ref[...])
        columns = slice(j * half, (j + 1) * half)
        planes_ref[:, columns] = (part * weight_ref[:, columns]).astype(BF16)


def gelu_slope(values):
    bell = jnp.exp(-0.5 * values * values) * (1.0 / math.sqrt(2.0 * math.pi))
    return 0.5 * (1.0 + lax.erf(values * (1.0 / math.sqrt(2.0)))) + values * bell


def iota(shape, axis):
    return lax.broadcasted_iota(jnp.int32, shape, axis)


def forward_kernel(own, rest, count, s_ref, fields_hbm, basis_hbm, line_hbm, flat_ref, *refs):
    outs, refs = refs[:count], refs[count:]
    fields_ref, basis_ref, line_ref, fields_sem, basis_sem, line_sem = refs
    rows, _, _ = fields_ref.shape
    parts = fields_sem.shape[0]
    part = rows // parts
    pieces = basis_sem.shape[0]
    piece = basis_ref.shape[0] // pieces
    fields = [
        pltpu.make_async_copy(
            fields_hbm.at[pl.ds(k * part, part)], fields_ref.at[pl.ds(k * part, part)], fields_sem.at[k]
        )
        for k in range(parts)
    ]
    basis = [
        pltpu.make_async_copy(
            basis_hbm.at[pl.ds(k * piece, piece)], basis_ref.at[pl.ds(k * piece, piece)], basis_sem.at[k]
        )
        for k in range(pieces)
    ]
    line = pltpu.make_async_copy(line_hbm.at[s_ref[0]], line_ref, line_sem)
    for copy in fields + basis + [line]:
        copy.start()
    for k, copy in enumerate(fields):
        copy.wait()
        spread_rows(fields_ref, flat_ref, k * part, part)
    total = None
    for k, copy in enumerate(basis):
        copy.wait()
        span = slice(k * piece, (k + 1) * piece)
        term = dot(flat_ref[:, span], basis_ref[span])
        total = term if total is None else total + term
    line.wait()
    emit_modes(line_forward(total.astype(BF16), line_ref[...]), outs, own, rest)


def prepare_kernel(planes, part, cot_hbm, weight_hbm, flat_ref, channel_ref, bias_ref, *refs):
    out_ref, local_ref, down_ref, weight_ref, cot_ref, sem = refs
    cot_copy = pltpu.make_async_copy(cot_hbm, cot_ref, sem.at[0])
    cot_copy.start()
    weight_copy = pltpu.make_async_copy(weight_hbm, weight_ref, sem.at[1])
    weight_copy.start()
    rows, columns = flat_ref.shape
    chans = rows // planes
    row = iota((rows, chans), 0)
    column = iota((rows, chans), 1)
    member = (row >= column * planes) & (row < (column + 1) * planes)
    spread = jnp.where(member, 1.0, 0.0).astype(BF16)
    same = lax.rem(iota((rows, rows), 0), planes) == lax.rem(iota((rows, rows), 1), planes)
    channel = channel_ref[...]
    up = dot_nt(dot(spread, channel).astype(BF16), spread)
    down = dot_nt(dot_nt(spread, channel).astype(BF16), spread)
    up = jnp.where(same, up, 0.0).astype(BF16)
    down_ref[...] = jnp.where(same, down, 0.0).astype(BF16)
    bias = jnp.sum(jnp.where(member, bias_ref[...], 0.0), axis=1, keepdims=True)
    step = 8 * LANES
    for k in range(columns // step):
        span = slice(k * step, (k + 1) * step)
        local_ref[:, span] = dot(up, flat_ref[:, span]) + bias
    cot_copy.wait()
    for k in range(rows // part):
        spread_rows(cot_ref, out_ref, k * part, part)
    weight_copy.wait()


def sum_modes(mode_refs, scale, total_ref, out_ref, own):
    for blk in range(own + 1):
        total = mode_refs[0][blk]
        for ref in mode_refs[1:]:
            total = total + ref[blk].astype(F32)
        total = total * scale
        total_ref[blk] = total
        out_ref[blk] = total.astype(BF16)


def load_wide(total_ref, wide_ref, a, own, rest):
    wide_ref[:, :LANES] = total_ref[a]
    wide_ref[:, LANES:] = pltpu.roll(total_ref[own], lax.rem(LANES - a * rest, LANES), 1)


def store_wide(wide_ref, tail_ref, out_ref, a, own, rest):
    out_ref[a] = wide_ref[:, :LANES].astype(BF16)
    moved = pltpu.roll(wide_ref[:, LANES:], a * rest, 1)
    height = moved.shape[0]
    tail_ref[...] = jnp.where(tail_mask(a, height, rest), moved, tail_ref[...])

    @pl.when(a == own - 1)
    def _():
        out_ref[own] = tail_ref[...].astype(BF16)


def mix_kernel(own, rest, count, scale, *refs):
    refs = refs[1:]
    modes, (weight_ref, out_ref, sum_ref) = refs[:count], refs[count : count + 3]
    total_ref, wide_ref, result_ref, tail_ref = refs[count + 3 :]
    chans = weight_ref.shape[2]
    pairs = weight_ref.shape[4]
    sum_modes(modes, scale, total_ref, sum_ref, own)
    result_ref[...] = jnp.zeros_like(result_ref)
    tail_ref[...] = jnp.zeros_like(tail_ref)

    @pl.loop(0, own)
    def _(a):
        load_wide(total_ref, wide_ref, a, own, rest)
        real = jnp.zeros((chans, pairs), F32)
        imag = jnp.zeros((chans, pairs), F32)
        for i in range(chans):
            w_real = weight_ref[a, 0, i].astype(F32)
            w_imag = weight_ref[a, 1, i].astype(F32)
            u_real = wide_ref[i : i + 1, :pairs]
            u_imag = wide_ref[chans + i : chans + i + 1, :pairs]
            real = real + (w_real * u_real - w_imag * u_imag)
            imag = imag + (w_real * u_imag + w_imag * u_real)
        result_ref[:chans, :pairs] = real
        result_ref[chans:, :pairs] = imag
        store_wide(result_ref, tail_ref, out_ref, a, own, rest)


def total_kernel(own, count, *refs):
    modes, (chan_ref, total_ref, sum_ref) = refs[:count], refs[count:]
    chans = chan_ref.shape[0]
    sum_modes(modes, 1.0, total_ref, sum_ref, own)
    chan = chan_ref[...]
    for ref in modes[1:]:
        chan = chan + (ref[own + 1, :chans].astype(F32) + ref[own + 1, chans:].astype(F32))
    upper = chan.astype(BF16)
    sum_ref[own + 1, :chans] = upper
    sum_ref[own + 1, chans:] = (chan - upper.astype(F32)).astype(BF16)


def mix_back_kernel(own, rest, ties, *refs):
    total_ref, weight_ref, out_ref, wide_ref, result_ref, tail_ref, part_ref = refs[ties:]
    chans = weight_ref.shape[2]
    pairs = weight_ref.shape[4]
    group = 8
    result_ref[...] = jnp.zeros_like(result_ref)
    tail_ref[...] = jnp.zeros_like(tail_ref)

    @pl.loop(0, own)
    def _(a):
        load_wide(total_ref, wide_ref, a, own, rest)
        g_real = wide_ref[:chans, :pairs]
        g_imag = wide_ref[chans:, :pairs]
        for i in range(chans):
            w_real = weight_ref[a, 0, i].astype(F32)
            w_imag = weight_ref[a, 1, i].astype(F32)
            real = w_real * g_real + w_imag * g_imag
            imag = w_real * g_imag - w_imag * g_real
            real = sum(real[k : k + group] for k in range(0, chans, group))
            imag = sum(imag[k : k + group] for k in range(0, chans, group))
            for r, value in enumerate((real, imag)):
                first = (r * chans + i) * group
                part_ref[0, first : first + group, :] = value[:, :LANES]
                part_ref[1, first : first + group, : pairs - LANES] = value[:, LANES:]
        for half in range(2):
            rows = [part_ref[half, pl.ds(k, 2 * chans, stride=group), :] for k in range(group)]
            result_ref[:, half * LANES : (half + 1) * LANES] = sum(rows[1:], rows[0])
        store_wide(result_ref, tail_ref, out_ref, a, own, rest)


def middle_kernel(own, rest, count, planes, ties, s_ref, *refs):
    refs = refs[ties:]
    modes, refs = refs[:count], refs[count:]
    inverse_ref, line_ref, weight_ref, flat_ref, cot_ref, local_ref, basis_ref = refs[:7]
    hidden_ref, chan_ref, refs = refs[7], refs[8], refs[9:]
    outs, (stack_ref, planes_ref) = refs[:count], refs[count:]
    planes_of(modes, inverse_ref[s_ref[0]], weight_ref, stack_ref, planes_ref, own, rest)
    rows, columns = flat_ref.shape
    step = 4 * LANES
    back = jnp.zeros((rows, weight_ref.shape[1]), F32)
    cross = jnp.zeros((rows, rows), F32)
    for k in range(columns // step):
        span = slice(k * step, (k + 1) * step)
        summed = dot_nt(planes_ref[...], basis_ref[span]) + local_ref[:, span]
        hidden = (cot_ref[:, span].astype(F32) * gelu_slope(summed)).astype(BF16)
        hidden_ref[:, span] = hidden
        back = back + dot(hidden, basis_ref[span])
        cross = cross + dot_nt(hidden, flat_ref[:, span])
    spec = (back * weight_ref[...]).astype(BF16)
    emit_modes(line_forward(spec, line_ref[s_ref[0]]), outs, own, rest)
    chans = rows // planes
    same = lax.rem(iota((rows, rows), 0), planes) == lax.rem(iota((rows, rows), 1), planes)
    cross = jnp.where(same, cross, 0.0)
    row, column = iota((chans, rows), 0), iota((chans, rows), 1)
    group = jnp.where((column >= row * planes) & (column < (row + 1) * planes), 1.0, 0.0)
    row, column = iota((rows, LANES), 0), iota((rows, LANES), 1)
    place = jnp.where((row >= column * planes) & (row < (column + 1) * planes), 1.0, 0.0)
    exact = functools.partial(jnp.dot, preferred_element_type=F32, precision=lax.Precision.HIGHEST)
    sums = jnp.where(column == chans, back[:, :1], 0.0)
    chan = exact(group, exact(cross, place) + sums)
    chan_ref[...] = chan
    upper = chan.astype(BF16)
    lower = (chan - upper.astype(F32)).astype(BF16)
    for ref in outs[1:]:
        ref[own + 1, :chans] = upper
        ref[own + 1, chans:] = lower


def last_kernel(own, rest, count, part, ties, s_ref, *refs):
    refs = refs[ties:]
    modes, refs = refs[:count], refs[count:]
    inverse_ref, weight_ref, mix_ref, hidden_ref, basis_ref, out_hbm = refs[:6]
    stack_ref, planes_ref, turned_ref, out_ref, sem = refs[6:]
    rows, ny_len, nz_len = out_ref.shape
    planes_of(modes, inverse_ref[s_ref[0]], weight_ref, stack_ref, planes_ref, own, rest)
    group = 4
    step = group * nz_len
    for k in range(ny_len // group):
        span = slice(k * step, (k + 1) * step)
        total = dot_nt(planes_ref[...], basis_ref[span]) + dot(mix_ref[...], hidden_ref[:, span])
        total = total.astype(BF16)
        for y in range(group):
            turned_ref[k * group + y] = total[:, y * nz_len : (y + 1) * nz_len]
    copies = []
    for k in range(rows // part):
        span = slice(k * part, (k + 1) * part)
        out_ref[span] = jnp.swapaxes(turned_ref[:, span], 0, 1)
        here = pl.ds(k * part, part)
        copies.append(pltpu.make_async_copy(out_ref.at[here], out_hbm.at[here], sem.at[k]))
        copies[-1].start()
    for copy in copies:
        copy.wait()


def load_cells(u_refs, g_refs, blk, u_all, g_all, factor):
    chans = g_all.shape[2]
    for b, (u_ref, g_ref) in enumerate(zip(u_refs, g_refs, strict=True)):
        g_real = g_ref[blk, :chans].astype(F32)
        g_imag = g_ref[blk, chans:].astype(F32)
        u_real = u_ref[blk, :chans].astype(F32) * factor
        u_imag = u_ref[blk, chans:].astype(F32) * factor
        g_all[b, 0] = g_real + g_imag
        g_all[b, 1] = g_real
        g_all[b, 2] = g_imag
        u_all[b, 0] = u_real
        u_all[b, 1] = u_real + u_imag
        u_all[b, 2] = u_real - u_imag


TOGETHER = 4


def products(u_all, g_all, first):
    sums = [[None] * 3 for _ in range(TOGETHER)]
    for b in range(u_all.shape[0]):
        for t in range(3):
            grad = g_all[b, t]
            for k in range(TOGETHER):
                term = u_all[b, t, pl.ds(first + k, 1), :] * grad
                sums[k][t] = term if sums[k][t] is None else sums[k][t] + term
    return [(part[0] - part[2], part[0] - part[1]) for part in sums]


def tag_sum(refs, at, chans):
    total = jnp.zeros((chans, LANES), F32)
    for ref in refs:
        total = total + (ref[at, :chans].astype(F32) + ref[at, chans:].astype(F32))
    return total


def early_kernel(cells, ties, factor, *refs):
    refs = refs[ties:]
    u_refs, g_refs = refs[:cells], refs[cells : 2 * cells]
    out_ref, chan_ref, u_all, g_all = refs[2 * cells :]
    chans = g_all.shape[2]
    chan_ref[...] = tag_sum(g_refs, out_ref.shape[0], chans)

    @pl.loop(0, out_ref.shape[0])
    def _(blk):
        load_cells(u_refs, g_refs, blk, u_all, g_all, factor)

        @pl.loop(0, chans, step=TOGETHER)
        def _(i):
            for k, parts in enumerate(products(u_all, g_all, i)):
                for r, part in enumerate(parts):
                    out_ref[blk, r, i + k] = part.astype(BF16)


def outer_kernel(rest, cells, sums, factor, norm, *refs):
    u_refs, g_refs, refs = refs[:cells], refs[cells : 2 * cells], refs[2 * cells :]
    sum_refs, sum_chans, refs = refs[:sums], refs[sums : 2 * sums], refs[2 * sums :]
    out_ref, chan_ref, bias_ref, u_all, g_all, tail_ref = refs
    step = pl.program_id(0)
    own = pl.num_programs(0) - 1
    blk = jnp.where(step == 0, own, step - 1)
    chans = g_all.shape[2]
    load_cells(u_refs, g_refs, blk, u_all, g_all, factor)

    def totals(i):
        for k, parts in enumerate(products(u_all, g_all, i)):
            for r, part in enumerate(parts):
                for ref in sum_refs:
                    part = part + ref[blk, r, i + k].astype(F32)
                yield r, i + k, part

    @pl.when(step == 0)
    def _():
        chan = tag_sum(g_refs, own + 1, chans)
        for ref in sum_chans:
            chan = chan + ref[...]
        chan = chan * norm
        chan_ref[...] = chan[:, :chans]
        same = iota((chans, LANES), 0) == iota((chans, LANES), 1)
        bias = jnp.sum(jnp.where(same, chan[:, chans : chans + 1], 0.0), axis=0, keepdims=True)
        bias_ref[...] = bias[:, :chans]

        @pl.loop(0, chans, step=TOGETHER, unroll=2)
        def _(i):
            for r, at, part in totals(i):
                tail_ref[r, at] = part

    @pl.when(step > 0)
    def _():
        shift = lax.rem(LANES - (step - 1) * rest, LANES)

        @pl.loop(0, chans, step=TOGETHER, unroll=2)
        def _(i):
            for r, at, part in totals(i):
                out_ref[0, r, at, :, :LANES] = part
                out_ref[0, r, at, :, LANES:] = pltpu.roll(tail_ref[r, at], shift, 1)[:, :rest]


def about(microseconds):
    return pl.CostEstimate(
        flops=int(microseconds * 1.15e9), bytes_accessed=int(microseconds * 3.6e6), transcendentals=0
    )


def call(kernel, name, time, ins, outs, scratch=(), limit=16):
    return pl.pallas_call(
        kernel,
        in_specs=ins,
        out_specs=[pl.BlockSpec(memory_space=out[2] if len(out) > 2 else pltpu.VMEM) for out in outs],
        out_shape=[jax.ShapeDtypeStruct(*out[:2]) for out in outs],
        scratch_shapes=list(scratch),
        compiler_params=pltpu.CompilerParams(vmem_limit_bytes=limit * 1024 * 1024),
        cost_estimate=about(time),
        name=name,
    )


def here(number):
    return [pl.BlockSpec(memory_space=pltpu.VMEM)] * number


def there(number):
    return [pl.BlockSpec(memory_space=pltpu.HBM)] * number


def send(array, axis, count, shift):
    return lax.ppermute(array, axis, [(i, (i + shift) % count) for i in range(count)])


def swap(array, bit, count):
    return lax.ppermute(array, "dp", [(i, i ^ bit) for i in range(count)])


def first_cells(array, count):
    if count & (count - 1) or count < 8:
        return []
    return [array, swap(array, 2, count)] + [swap(array, 4 * z, count) for z in range(1, count // 4)]


def order_cells(array, first, count):
    if not first:
        return [], list(lax.all_gather(array, "dp"))
    near = first[:2] + [piece for far in first[2:] for piece in (far, swap(far, 2, count))]
    return near[: len(near) // 2], near[len(near) // 2 :]


def scratch_cells(cells, chans):
    return [pltpu.VMEM((cells, 3, chans, LANES), F32)] * 2


def early_gradient(all_u, all_g, ties, own, cell_norm):
    cells = len(all_u)
    chans = all_u[0].shape[1] // 2
    return call(
        functools.partial(early_kernel, cells, len(ties), cell_norm),
        "early",
        4.8,
        there(len(ties)) + here(2 * cells),
        [((own + 1, 2, chans, chans, LANES), BF16), ((chans, LANES), F32)],
        scratch_cells(cells, chans),
    )(*ties, *all_u, *all_g)


def weight_gradient(all_u, all_g, sums, weight_shape, norms):
    own, _, chans, _, pairs = weight_shape
    cell_norm, voxel_norm = norms
    cells = len(all_u)
    half = len(sums) // 2
    return pl.pallas_call(
        functools.partial(outer_kernel, pairs - LANES, cells, half, cell_norm, voxel_norm),
        grid=(own + 1,),
        in_specs=here(2 * cells + 2 * half),
        out_specs=[
            pl.BlockSpec((1,) + weight_shape[1:], lambda i: (jnp.maximum(i - 1, 0), 0, 0, 0, 0)),
            pl.BlockSpec((chans, chans), lambda i: (0, 0)),
            pl.BlockSpec((1, chans), lambda i: (0, 0)),
        ],
        out_shape=[
            jax.ShapeDtypeStruct(weight_shape, F32),
            jax.ShapeDtypeStruct((chans, chans), F32),
            jax.ShapeDtypeStruct((1, chans), F32),
        ],
        scratch_shapes=scratch_cells(cells, chans) + [pltpu.VMEM((2, chans, chans, LANES), F32)],
        compiler_params=pltpu.CompilerParams(vmem_limit_bytes=20 * 1024 * 1024),
        cost_estimate=about(12.8),
        name="outer",
    )(*all_u, *all_g, *sums)


def shards(count, cell_count, fields, cotangent, spectral_weight, channel_weight, channel_bias):
    _, chans, planes, ny_len, nz_len = fields.shape
    own, _, _, _, pairs = spectral_weight.shape
    rest = pairs - LANES
    rows = chans * planes
    columns = ny_len * nz_len
    block = min(rows, 64)
    scale = 1.0 / math.sqrt(planes * count * columns)
    cell_norm = 1.0 / math.sqrt(cell_count)
    voxel_norm = 1.0 / math.sqrt(cell_count * planes * count * columns)
    height = 2 * chans
    wide = 4 * LANES

    basis = jnp.asarray(plane_table(ny_len, nz_len, own))
    line_np = line_tables(chans, planes, count)
    line = jnp.asarray(line_np)
    inverse = jnp.asarray(np.ascontiguousarray(np.swapaxes(line_np, 1, 2)))
    up_weight = jnp.asarray(column_weight(own, scale))
    down_weight = jnp.asarray(np.full((1, wide), scale, np.float32))
    place = lax.axis_index("space").astype(jnp.int32).reshape(1)

    modes = ((own + 1, height, LANES), F32)
    sent = ((own + 1, height, LANES), BF16)
    tagged = ((own + 2, height, LANES), BF16)
    grid_like = (rows, ny_len, nz_len)

    flat, mine, *others = call(
        functools.partial(forward_kernel, own, rest, count),
        "forward",
        4.3,
        [pl.BlockSpec(memory_space=pltpu.SMEM)] + there(3),
        [((rows, columns), BF16), modes] + [sent] * (count - 1),
        [
            pltpu.VMEM(grid_like, BF16),
            pltpu.VMEM(basis.shape, BF16),
            pltpu.VMEM(line.shape[1:], BF16),
            pltpu.SemaphoreType.DMA((rows // block,)),
            pltpu.SemaphoreType.DMA((5,)),
            pltpu.SemaphoreType.DMA,
        ],
        52,
    )(place, fields.reshape(grid_like), basis, line)
    arrived = [send(array, "space", count, k + 1) for k, array in enumerate(others)]
    cot, local, mix_down, weights = call(
        functools.partial(prepare_kernel, planes, block),
        "prepare",
        2.5,
        there(2) + here(3),
        [((rows, columns), BF16), ((rows, columns), F32), ((rows, rows), BF16), (spectral_weight.shape, BF16)],
        [pltpu.VMEM(grid_like, BF16), pltpu.SemaphoreType.DMA((2,))],
        28,
    )(cotangent.reshape(grid_like), spectral_weight, flat, channel_weight, channel_bias.reshape(1, chans))

    mix_scratch = [
        pltpu.VMEM((height, 2 * LANES), F32),
        pltpu.VMEM((height, 2 * LANES), F32),
        pltpu.VMEM((height, LANES), F32),
    ]
    mixed, field_modes = call(
        functools.partial(mix_kernel, own, rest, count, scale),
        "mix",
        3.9,
        there(1) + here(count + 1),
        [sent, sent],
        [pltpu.VMEM(modes[0], F32)] + mix_scratch,
    )(cot, mine, *arrived, weights)

    u_first = first_cells(field_modes, cell_count)
    ties = u_first[1:3]
    all_mixed = [mixed] + [send(mixed, "space", count, -k) for k in range(1, count)]
    plane_scratch = [pltpu.VMEM((count * own * height, 2 * LANES), BF16), pltpu.VMEM((rows, wide), BF16)]
    hidden, chan, mine, *others = call(
        functools.partial(middle_kernel, own, rest, count, planes, len(ties)),
        "middle",
        6.3,
        [pl.BlockSpec(memory_space=pltpu.SMEM)] + there(len(ties)) + here(count + 7),
        [((rows, columns), BF16), ((chans, LANES), F32), modes] + [tagged] * (count - 1),
        plane_scratch,
    )(place, *ties, *all_mixed, inverse, line, up_weight, flat, cot, local, basis)
    arrived = [send(array, "space", count, k + 1) for k, array in enumerate(others)]

    total, grad_modes = call(
        functools.partial(total_kernel, own, count), "total", 1.0, here(count + 1), [modes, tagged]
    )(mine, *arrived, chan)
    ties = u_first[3:]
    (returned,) = call(
        functools.partial(mix_back_kernel, own, rest, len(ties)),
        "mix_back",
        4.1,
        there(len(ties)) + here(2),
        [sent],
        mix_scratch + [pltpu.VMEM((2, 2 * chans * 8, LANES), F32)],
    )(*ties, total, weights)

    g_first = first_cells(grad_modes, cell_count)
    all_returned = [returned] + [send(returned, "space", count, -k) for k in range(1, count)]
    early_u, late_u = order_cells(field_modes, u_first, cell_count)
    early_g, late_g = order_cells(grad_modes, g_first, cell_count)
    sums = []
    if early_u:
        late_u = late_u + [swap(piece, 1, cell_count) for piece in late_u]
        ties = all_returned + g_first[3:] + late_u
        part, part_chan = early_gradient(early_u, early_g, ties, own, cell_norm)
        sums = [part, swap(part, 1, cell_count), part_chan, swap(part_chan, 1, cell_count)]
        late_g = late_g + [swap(piece, 1, cell_count) for piece in late_g]
    ties = sums[:1]
    (grad_fields,) = call(
        functools.partial(last_kernel, own, rest, count, block, len(ties)),
        "last",
        4.4,
        [pl.BlockSpec(memory_space=pltpu.SMEM)] + there(len(ties)) + here(count + 5),
        [(grid_like, BF16, pltpu.HBM)],
        plane_scratch
        + [
            pltpu.VMEM((ny_len, rows, nz_len), BF16),
            pltpu.VMEM(grid_like, BF16),
            pltpu.SemaphoreType.DMA((rows // block,)),
        ],
    )(place, *ties, *all_returned, inverse, down_weight, mix_down, hidden, basis)

    grad_spectral, grad_channel, grad_bias = weight_gradient(
        late_u, late_g, sums, spectral_weight.shape, (cell_norm, voxel_norm)
    )
    return (grad_fields.reshape(fields.shape), grad_spectral, grad_channel, grad_bias.reshape(chans))


def solution(mesh):
    in_specs = (
        P("dp", None, "space", None, None),
        P("dp", None, "space", None, None),
        P("space", None, None, None, None),
        P(),
        P(),
    )
    out_specs = (P("dp", None, "space", None, None), P("space", None, None, None, None), P(), P())
    body = functools.partial(shards, mesh.shape["space"], mesh.shape["dp"])
    return jax.shard_map(body, mesh=mesh, in_specs=in_specs, out_specs=out_specs, check_vma=False)
```

```python
import functools
import math

import jax
import jax.numpy as jnp
import ml_dtypes
import numpy as np
from jax import lax
from jax.experimental import pallas as pl
from jax.experimental.pallas import tpu as pltpu
from jax.sharding import PartitionSpec as P

MX = 16
MY = 16
MZ = 9
LANES = 128
BF16 = jnp.bfloat16
F32 = jnp.float32
TWO_PI = 2.0 * math.pi


def signed(index, modes):
    return np.where(index < modes // 2, index, index - modes)


def plane_columns(own):
    pairs = MY * MZ
    rest = pairs - LANES
    return np.concatenate([np.arange(LANES), LANES + np.tile(np.arange(rest), own)])


def plane_table(ny_len, nz_len, own):
    ky = signed(np.arange(MY), MY)
    kz = np.arange(MZ)
    y_pos = np.arange(ny_len)
    z_pos = np.arange(nz_len)
    phases = (
        y_pos[:, None, None, None] * ky[None, None, :, None] * nz_len
        + z_pos[None, :, None, None] * kz[None, None, None, :] * ny_len
    ) % (ny_len * nz_len)
    angles = phases.astype(np.float32) * np.float32(TWO_PI / (ny_len * nz_len))
    angles = angles.reshape(ny_len * nz_len, MY * MZ)
    columns = plane_columns(own)
    table = np.zeros((ny_len * nz_len, 2, 2 * LANES), np.float32)
    table[:, 0, : len(columns)] = np.cos(angles)[:, columns]
    table[:, 1, : len(columns)] = -np.sin(angles)[:, columns]
    return table.reshape(ny_len * nz_len, 4 * LANES).astype(ml_dtypes.bfloat16)


def column_weight(own, scale):
    columns = plane_columns(own)
    weight = np.zeros((2, 2 * LANES), np.float32)
    weight[:, : len(columns)] = np.where(columns % MZ == 0, 1.0, 2.0)
    return (weight * scale).reshape(1, 4 * LANES).astype(np.float32)


def line_tables(chans, planes, count):
    own = MX // count
    length = planes * count
    tables = []
    for s in range(count):
        place = (s + np.arange(count)) % count
        index = (place[:, None] * own + np.arange(own)[None, :]).reshape(-1)
        phases = signed(index, MX)[:, None] * (s * planes + np.arange(planes))[None, :] % length
        angles = phases.astype(np.float32) * np.float32(TWO_PI / length)
        cosine, sines = np.cos(angles), np.sin(angles)
        line = np.stack([np.stack([cosine, sines], -1), np.stack([-sines, cosine], -1)], 1)
        whole = np.einsum("arxj,cd->arcjdx", line, np.eye(chans, dtype=np.float32))
        tables.append(whole.reshape(MX * 2 * chans, 2 * chans * planes))
    return np.stack(tables).astype(ml_dtypes.bfloat16)


def dot(left, right):
    return jnp.dot(left, right, preferred_element_type=F32)


def dot_nt(left, right):
    return lax.dot_general(left, right, (((1,), (1,)), ((), ())), preferred_element_type=F32)


def tail_mask(a, rows, rest):
    lane = lax.broadcasted_iota(jnp.int32, (rows, LANES), 1)
    return (lane >= a * rest) & (lane < (a + 1) * rest)


def spread_rows(block_ref, out_ref, start, count):
    _, ny_len, nz_len = block_ref.shape
    turned = jnp.swapaxes(block_ref[start : start + count], 0, 1)
    for y in range(ny_len):
        out_ref[start : start + count, y * nz_len : (y + 1) * nz_len] = turned[y]


def emit_modes(terms, refs, own, rest):
    height = terms.shape[0] // (own * len(refs))
    for k, ref in enumerate(refs):
        tail = jnp.zeros((height, LANES), F32)
        for a in range(own):
            first = (k * own + a) * height
            block = terms[first : first + height]
            ref[a] = block[:, :LANES].astype(ref.dtype)
            tail = jnp.where(tail_mask(a, height, rest), block[:, LANES:], tail)
        ref[own] = tail.astype(ref.dtype)


def line_forward(spec, line):
    half = 2 * LANES
    depth = line.shape[1] // 2
    return dot(line[:, :depth], spec[:, :half]) + dot(line[:, depth:], spec[:, half:])


def planes_of(mode_refs, inverse, weight_ref, stack_ref, planes_ref, own, rest):
    height = mode_refs[0].shape[1]
    half = 2 * LANES
    for k, ref in enumerate(mode_refs):
        tail = ref[own].astype(F32)
        for a in range(own):
            first = (k * own + a) * height
            stack_ref[first : first + height, :LANES] = ref[a]
            masked = jnp.where(tail_mask(a, height, rest), tail, 0.0)
            stack_ref[first : first + height, LANES:] = masked.astype(BF16)
    depth = inverse.shape[0] // 2
    for j in range(2):
        part = dot(inverse[j * depth : (j + 1) * depth, :], stack_ref[...])
        columns = slice(j * half, (j + 1) * half)
        planes_ref[:, columns] = (part * weight_ref[:, columns]).astype(BF16)


def gelu_slope(values):
    bell = jnp.exp(-0.5 * values * values) * (1.0 / math.sqrt(2.0 * math.pi))
    return 0.5 * (1.0 + lax.erf(values * (1.0 / math.sqrt(2.0)))) + values * bell


def iota(shape, axis):
    return lax.broadcasted_iota(jnp.int32, shape, axis)


def forward_kernel(own, rest, count, s_ref, fields_hbm, basis_hbm, line_hbm, flat_ref, *refs):
    outs, refs = refs[:count], refs[count:]
    fields_ref, basis_ref, line_ref, fields_sem, basis_sem, line_sem = refs
    rows, _, _ = fields_ref.shape
    parts = fields_sem.shape[0]
    part = rows // parts
    pieces = basis_sem.shape[0]
    piece = basis_ref.shape[0] // pieces
    fields = [
        pltpu.make_async_copy(
            fields_hbm.at[pl.ds(k * part, part)], fields_ref.at[pl.ds(k * part, part)], fields_sem.at[k]
        )
        for k in range(parts)
    ]
    basis = [
        pltpu.make_async_copy(
            basis_hbm.at[pl.ds(k * piece, piece)], basis_ref.at[pl.ds(k * piece, piece)], basis_sem.at[k]
        )
        for k in range(pieces)
    ]
    line = pltpu.make_async_copy(line_hbm.at[s_ref[0]], line_ref, line_sem)
    for copy in fields + basis + [line]:
        copy.start()
    for k, copy in enumerate(fields):
        copy.wait()
        spread_rows(fields_ref, flat_ref, k * part, part)
    total = None
    for k, copy in enumerate(basis):
        copy.wait()
        span = slice(k * piece, (k + 1) * piece)
        term = dot(flat_ref[:, span], basis_ref[span])
        total = term if total is None else total + term
    line.wait()
    emit_modes(line_forward(total.astype(BF16), line_ref[...]), outs, own, rest)


def prepare_kernel(planes, part, cot_hbm, weight_hbm, flat_ref, channel_ref, bias_ref, *refs):
    out_ref, local_ref, down_ref, weight_ref, cot_ref, sem = refs
    cot_copy = pltpu.make_async_copy(cot_hbm, cot_ref, sem.at[0])
    cot_copy.start()
    weight_copy = pltpu.make_async_copy(weight_hbm, weight_ref, sem.at[1])
    weight_copy.start()
    rows, columns = flat_ref.shape
    chans = rows // planes
    row = iota((rows, chans), 0)
    column = iota((rows, chans), 1)
    member = (row >= column * planes) & (row < (column + 1) * planes)
    spread = jnp.where(member, 1.0, 0.0).astype(BF16)
    same = lax.rem(iota((rows, rows), 0), planes) == lax.rem(iota((rows, rows), 1), planes)
    channel = channel_ref[...]
    up = dot_nt(dot(spread, channel).astype(BF16), spread)
    down = dot_nt(dot_nt(spread, channel).astype(BF16), spread)
    up = jnp.where(same, up, 0.0).astype(BF16)
    down_ref[...] = jnp.where(same, down, 0.0).astype(BF16)
    bias = jnp.sum(jnp.where(member, bias_ref[...], 0.0), axis=1, keepdims=True)
    step = 8 * LANES
    for k in range(columns // step):
        span = slice(k * step, (k + 1) * step)
        local_ref[:, span] = dot(up, flat_ref[:, span]) + bias
    cot_copy.wait()
    for k in range(rows // part):
        spread_rows(cot_ref, out_ref, k * part, part)
    weight_copy.wait()


def sum_modes(mode_refs, scale, total_ref, out_ref, own):
    for blk in range(own + 1):
        total = mode_refs[0][blk]
        for ref in mode_refs[1:]:
            total = total + ref[blk].astype(F32)
        total = total * scale
        total_ref[blk] = total
        out_ref[blk] = total.astype(BF16)


def load_wide(total_ref, wide_ref, a, own, rest):
    wide_ref[:, :LANES] = total_ref[a]
    wide_ref[:, LANES:] = pltpu.roll(total_ref[own], lax.rem(LANES - a * rest, LANES), 1)


def store_wide(wide_ref, tail_ref, out_ref, a, own, rest):
    out_ref[a] = wide_ref[:, :LANES].astype(BF16)
    moved = pltpu.roll(wide_ref[:, LANES:], a * rest, 1)
    height = moved.shape[0]
    tail_ref[...] = jnp.where(tail_mask(a, height, rest), moved, tail_ref[...])

    @pl.when(a == own - 1)
    def _():
        out_ref[own] = tail_ref[...].astype(BF16)


def mix_kernel(own, rest, count, scale, *refs):
    refs = refs[1:]
    modes, (weight_ref, out_ref, sum_ref) = refs[:count], refs[count : count + 3]
    total_ref, wide_ref, result_ref, tail_ref = refs[count + 3 :]
    chans = weight_ref.shape[2]
    pairs = weight_ref.shape[4]
    sum_modes(modes, scale, total_ref, sum_ref, own)
    result_ref[...] = jnp.zeros_like(result_ref)
    tail_ref[...] = jnp.zeros_like(tail_ref)

    @pl.loop(0, own)
    def _(a):
        load_wide(total_ref, wide_ref, a, own, rest)
        real = jnp.zeros((chans, pairs), F32)
        imag = jnp.zeros((chans, pairs), F32)
        for i in range(chans):
            w_real = weight_ref[a, 0, i].astype(F32)
            w_imag = weight_ref[a, 1, i].astype(F32)
            u_real = wide_ref[i : i + 1, :pairs]
            u_imag = wide_ref[chans + i : chans + i + 1, :pairs]
            real = real + (w_real * u_real - w_imag * u_imag)
            imag = imag + (w_real * u_imag + w_imag * u_real)
        result_ref[:chans, :pairs] = real
        result_ref[chans:, :pairs] = imag
        store_wide(result_ref, tail_ref, out_ref, a, own, rest)


def total_kernel(own, count, *refs):
    modes, (chan_ref, total_ref, sum_ref) = refs[:count], refs[count:]
    chans = chan_ref.shape[0]
    sum_modes(modes, 1.0, total_ref, sum_ref, own)
    chan = chan_ref[...]
    for ref in modes[1:]:
        chan = chan + (ref[own + 1, :chans].astype(F32) + ref[own + 1, chans:].astype(F32))
    upper = chan.astype(BF16)
    sum_ref[own + 1, :chans] = upper
    sum_ref[own + 1, chans:] = (chan - upper.astype(F32)).astype(BF16)


def mix_back_kernel(own, rest, ties, *refs):
    total_ref, weight_ref, out_ref, wide_ref, result_ref, tail_ref, part_ref = refs[ties:]
    chans = weight_ref.shape[2]
    pairs = weight_ref.shape[4]
    group = 8
    result_ref[...] = jnp.zeros_like(result_ref)
    tail_ref[...] = jnp.zeros_like(tail_ref)

    @pl.loop(0, own)
    def _(a):
        load_wide(total_ref, wide_ref, a, own, rest)
        g_real = wide_ref[:chans, :pairs]
        g_imag = wide_ref[chans:, :pairs]
        for i in range(chans):
            w_real = weight_ref[a, 0, i].astype(F32)
            w_imag = weight_ref[a, 1, i].astype(F32)
            real = w_real * g_real + w_imag * g_imag
            imag = w_real * g_imag - w_imag * g_real
            real = sum(real[k : k + group] for k in range(0, chans, group))
            imag = sum(imag[k : k + group] for k in range(0, chans, group))
            for r, value in enumerate((real, imag)):
                first = (r * chans + i) * group
                part_ref[0, first : first + group, :] = value[:, :LANES]
                part_ref[1, first : first + group, : pairs - LANES] = value[:, LANES:]
        for half in range(2):
            rows = [part_ref[half, pl.ds(k, 2 * chans, stride=group), :] for k in range(group)]
            result_ref[:, half * LANES : (half + 1) * LANES] = sum(rows[1:], rows[0])
        store_wide(result_ref, tail_ref, out_ref, a, own, rest)


def middle_kernel(own, rest, count, planes, ties, s_ref, *refs):
    refs = refs[ties:]
    modes, refs = refs[:count], refs[count:]
    inverse_ref, line_ref, weight_ref, flat_ref, cot_ref, local_ref, basis_ref = refs[:7]
    hidden_ref, chan_ref, refs = refs[7], refs[8], refs[9:]
    outs, (stack_ref, planes_ref) = refs[:count], refs[count:]
    planes_of(modes, inverse_ref[s_ref[0]], weight_ref, stack_ref, planes_ref, own, rest)
    rows, columns = flat_ref.shape
    step = 4 * LANES
    back = jnp.zeros((rows, weight_ref.shape[1]), F32)
    cross = jnp.zeros((rows, rows), F32)
    for k in range(columns // step):
        span = slice(k * step, (k + 1) * step)
        summed = dot_nt(planes_ref[...], basis_ref[span]) + local_ref[:, span]
        hidden = (cot_ref[:, span].astype(F32) * gelu_slope(summed)).astype(BF16)
        hidden_ref[:, span] = hidden
        back = back + dot(hidden, basis_ref[span])
        cross = cross + dot_nt(hidden, flat_ref[:, span])
    spec = (back * weight_ref[...]).astype(BF16)
    emit_modes(line_forward(spec, line_ref[s_ref[0]]), outs, own, rest)
    chans = rows // planes
    same = lax.rem(iota((rows, rows), 0), planes) == lax.rem(iota((rows, rows), 1), planes)
    cross = jnp.where(same, cross, 0.0)
    row, column = iota((chans, rows), 0), iota((chans, rows), 1)
    group = jnp.where((column >= row * planes) & (column < (row + 1) * planes), 1.0, 0.0)
    row, column = iota((rows, LANES), 0), iota((rows, LANES), 1)
    place = jnp.where((row >= column * planes) & (row < (column + 1) * planes), 1.0, 0.0)
    exact = functools.partial(jnp.dot, preferred_element_type=F32, precision=lax.Precision.HIGHEST)
    sums = jnp.where(column == chans, back[:, :1], 0.0)
    chan = exact(group, exact(cross, place) + sums)
    chan_ref[...] = chan
    upper = chan.astype(BF16)
    lower = (chan - upper.astype(F32)).astype(BF16)
    for ref in outs[1:]:
        ref[own + 1, :chans] = upper
        ref[own + 1, chans:] = lower


def last_kernel(own, rest, count, part, ties, s_ref, *refs):
    refs = refs[ties:]
    modes, refs = refs[:count], refs[count:]
    inverse_ref, weight_ref, mix_ref, hidden_ref, basis_ref, out_hbm = refs[:6]
    stack_ref, planes_ref, turned_ref, out_ref, sem = refs[6:]
    rows, ny_len, nz_len = out_ref.shape
    planes_of(modes, inverse_ref[s_ref[0]], weight_ref, stack_ref, planes_ref, own, rest)
    group = 4
    step = group * nz_len
    for k in range(ny_len // group):
        span = slice(k * step, (k + 1) * step)
        total = dot_nt(planes_ref[...], basis_ref[span]) + dot(mix_ref[...], hidden_ref[:, span])
        total = total.astype(BF16)
        for y in range(group):
            turned_ref[k * group + y] = total[:, y * nz_len : (y + 1) * nz_len]
    copies = []
    for k in range(rows // part):
        span = slice(k * part, (k + 1) * part)
        out_ref[span] = jnp.swapaxes(turned_ref[:, span], 0, 1)
        here = pl.ds(k * part, part)
        copies.append(pltpu.make_async_copy(out_ref.at[here], out_hbm.at[here], sem.at[k]))
        copies[-1].start()
    for copy in copies:
        copy.wait()


def load_cells(u_refs, g_refs, blk, u_all, g_all, factor):
    chans = g_all.shape[2]
    for b, (u_ref, g_ref) in enumerate(zip(u_refs, g_refs, strict=True)):
        g_real = g_ref[blk, :chans].astype(F32)
        g_imag = g_ref[blk, chans:].astype(F32)
        u_real = u_ref[blk, :chans].astype(F32) * factor
        u_imag = u_ref[blk, chans:].astype(F32) * factor
        g_all[b, 0] = g_real + g_imag
        g_all[b, 1] = g_real
        g_all[b, 2] = g_imag
        u_all[b, 0] = u_real
        u_all[b, 1] = u_real + u_imag
        u_all[b, 2] = u_real - u_imag


TOGETHER = 4


def products(u_all, g_all, first):
    sums = [[None] * 3 for _ in range(TOGETHER)]
    for b in range(u_all.shape[0]):
        for t in range(3):
            grad = g_all[b, t]
            for k in range(TOGETHER):
                term = u_all[b, t, pl.ds(first + k, 1), :] * grad
                sums[k][t] = term if sums[k][t] is None else sums[k][t] + term
    return [(part[0] - part[2], part[0] - part[1]) for part in sums]


def tag_sum(refs, at, chans):
    total = jnp.zeros((chans, LANES), F32)
    for ref in refs:
        total = total + (ref[at, :chans].astype(F32) + ref[at, chans:].astype(F32))
    return total


def early_kernel(cells, ties, factor, *refs):
    refs = refs[ties:]
    u_refs, g_refs = refs[:cells], refs[cells : 2 * cells]
    out_ref, chan_ref, u_all, g_all = refs[2 * cells :]
    chans = g_all.shape[2]
    chan_ref[...] = tag_sum(g_refs, out_ref.shape[0], chans)

    @pl.loop(0, out_ref.shape[0])
    def _(blk):
        load_cells(u_refs, g_refs, blk, u_all, g_all, factor)

        @pl.loop(0, chans, step=TOGETHER, unroll=2)
        def _(i):
            for k, parts in enumerate(products(u_all, g_all, i)):
                for r, part in enumerate(parts):
                    out_ref[blk, r, i + k] = part.astype(BF16)


def outer_kernel(rest, cells, sums, factor, norm, *refs):
    u_refs, g_refs, refs = refs[:cells], refs[cells : 2 * cells], refs[2 * cells :]
    sum_refs, sum_chans, refs = refs[:sums], refs[sums : 2 * sums], refs[2 * sums :]
    out_ref, chan_ref, bias_ref, u_all, g_all, tail_ref = refs
    step = pl.program_id(0)
    own = pl.num_programs(0) - 1
    blk = jnp.where(step == 0, own, step - 1)
    chans = g_all.shape[2]
    load_cells(u_refs, g_refs, blk, u_all, g_all, factor)

    def totals(i):
        for k, parts in enumerate(products(u_all, g_all, i)):
            for r, part in enumerate(parts):
                for ref in sum_refs:
                    part = part + ref[blk, r, i + k].astype(F32)
                yield r, i + k, part

    @pl.when(step == 0)
    def _():
        chan = tag_sum(g_refs, own + 1, chans)
        for ref in sum_chans:
            chan = chan + ref[...]
        chan = chan * norm
        chan_ref[...] = chan[:, :chans]
        same = iota((chans, LANES), 0) == iota((chans, LANES), 1)
        bias = jnp.sum(jnp.where(same, chan[:, chans : chans + 1], 0.0), axis=0, keepdims=True)
        bias_ref[...] = bias[:, :chans]

        @pl.loop(0, chans, step=TOGETHER, unroll=2)
        def _(i):
            for r, at, part in totals(i):
                tail_ref[r, at] = part

    @pl.when(step > 0)
    def _():
        shift = lax.rem(LANES - (step - 1) * rest, LANES)

        @pl.loop(0, chans, step=TOGETHER, unroll=2)
        def _(i):
            for r, at, part in totals(i):
                out_ref[0, r, at, :, :LANES] = part
                out_ref[0, r, at, :, LANES:] = pltpu.roll(tail_ref[r, at], shift, 1)[:, :rest]


def about(microseconds):
    return pl.CostEstimate(
        flops=int(microseconds * 1.15e9), bytes_accessed=int(microseconds * 3.6e6), transcendentals=0
    )


def call(kernel, name, time, ins, outs, scratch=(), limit=16):
    return pl.pallas_call(
        kernel,
        in_specs=ins,
        out_specs=[pl.BlockSpec(memory_space=out[2] if len(out) > 2 else pltpu.VMEM) for out in outs],
        out_shape=[jax.ShapeDtypeStruct(*out[:2]) for out in outs],
        scratch_shapes=list(scratch),
        compiler_params=pltpu.CompilerParams(vmem_limit_bytes=limit * 1024 * 1024),
        cost_estimate=about(time),
        name=name,
    )


def here(number):
    return [pl.BlockSpec(memory_space=pltpu.VMEM)] * number


def there(number):
    return [pl.BlockSpec(memory_space=pltpu.HBM)] * number


def send(array, axis, count, shift):
    return lax.ppermute(array, axis, [(i, (i + shift) % count) for i in range(count)])


def swap(array, bit, count):
    return lax.ppermute(array, "dp", [(i, i ^ bit) for i in range(count)])


def first_cells(array, count):
    if count & (count - 1) or count < 8:
        return []
    return [array, swap(array, 2, count)] + [swap(array, 4 * z, count) for z in range(1, count // 4)]


def order_cells(array, first, count):
    if not first:
        return [], list(lax.all_gather(array, "dp"))
    near = first[:2] + [piece for far in first[2:] for piece in (far, swap(far, 2, count))]
    return near[: len(near) // 2], near[len(near) // 2 :]


def scratch_cells(cells, chans):
    return [pltpu.VMEM((cells, 3, chans, LANES), F32)] * 2


def early_gradient(all_u, all_g, ties, own, cell_norm):
    cells = len(all_u)
    chans = all_u[0].shape[1] // 2
    return call(
        functools.partial(early_kernel, cells, len(ties), cell_norm),
        "early",
        4.8,
        there(len(ties)) + here(2 * cells),
        [((own + 1, 2, chans, chans, LANES), BF16), ((chans, LANES), F32)],
        scratch_cells(cells, chans),
    )(*ties, *all_u, *all_g)


def weight_gradient(all_u, all_g, sums, weight_shape, norms):
    own, _, chans, _, pairs = weight_shape
    cell_norm, voxel_norm = norms
    cells = len(all_u)
    half = len(sums) // 2
    return pl.pallas_call(
        functools.partial(outer_kernel, pairs - LANES, cells, half, cell_norm, voxel_norm),
        grid=(own + 1,),
        in_specs=here(2 * cells + 2 * half),
        out_specs=[
            pl.BlockSpec((1,) + weight_shape[1:], lambda i: (jnp.maximum(i - 1, 0), 0, 0, 0, 0)),
            pl.BlockSpec((chans, chans), lambda i: (0, 0)),
            pl.BlockSpec((1, chans), lambda i: (0, 0)),
        ],
        out_shape=[
            jax.ShapeDtypeStruct(weight_shape, F32),
            jax.ShapeDtypeStruct((chans, chans), F32),
            jax.ShapeDtypeStruct((1, chans), F32),
        ],
        scratch_shapes=scratch_cells(cells, chans) + [pltpu.VMEM((2, chans, chans, LANES), F32)],
        compiler_params=pltpu.CompilerParams(vmem_limit_bytes=20 * 1024 * 1024),
        cost_estimate=about(12.8),
        name="outer",
    )(*all_u, *all_g, *sums)


def shards(count, cell_count, fields, cotangent, spectral_weight, channel_weight, channel_bias):
    _, chans, planes, ny_len, nz_len = fields.shape
    own, _, _, _, pairs = spectral_weight.shape
    rest = pairs - LANES
    rows = chans * planes
    columns = ny_len * nz_len
    block = min(rows, 64)
    scale = 1.0 / math.sqrt(planes * count * columns)
    cell_norm = 1.0 / math.sqrt(cell_count)
    voxel_norm = 1.0 / math.sqrt(cell_count * planes * count * columns)
    height = 2 * chans
    wide = 4 * LANES

    basis = jnp.asarray(plane_table(ny_len, nz_len, own))
    line_np = line_tables(chans, planes, count)
    line = jnp.asarray(line_np)
    inverse = jnp.asarray(np.ascontiguousarray(np.swapaxes(line_np, 1, 2)))
    up_weight = jnp.asarray(column_weight(own, scale))
    down_weight = jnp.asarray(np.full((1, wide), scale, np.float32))
    place = lax.axis_index("space").astype(jnp.int32).reshape(1)

    modes = ((own + 1, height, LANES), F32)
    sent = ((own + 1, height, LANES), BF16)
    tagged = ((own + 2, height, LANES), BF16)
    grid_like = (rows, ny_len, nz_len)

    flat, mine, *others = call(
        functools.partial(forward_kernel, own, rest, count),
        "forward",
        4.3,
        [pl.BlockSpec(memory_space=pltpu.SMEM)] + there(3),
        [((rows, columns), BF16), modes] + [sent] * (count - 1),
        [
            pltpu.VMEM(grid_like, BF16),
            pltpu.VMEM(basis.shape, BF16),
            pltpu.VMEM(line.shape[1:], BF16),
            pltpu.SemaphoreType.DMA((rows // block,)),
            pltpu.SemaphoreType.DMA((5,)),
            pltpu.SemaphoreType.DMA,
        ],
        52,
    )(place, fields.reshape(grid_like), basis, line)
    arrived = [send(array, "space", count, k + 1) for k, array in enumerate(others)]
    cot, local, mix_down, weights = call(
        functools.partial(prepare_kernel, planes, block),
        "prepare",
        2.5,
        there(2) + here(3),
        [((rows, columns), BF16), ((rows, columns), F32), ((rows, rows), BF16), (spectral_weight.shape, BF16)],
        [pltpu.VMEM(grid_like, BF16), pltpu.SemaphoreType.DMA((2,))],
        28,
    )(cotangent.reshape(grid_like), spectral_weight, flat, channel_weight, channel_bias.reshape(1, chans))

    mix_scratch = [
        pltpu.VMEM((height, 2 * LANES), F32),
        pltpu.VMEM((height, 2 * LANES), F32),
        pltpu.VMEM((height, LANES), F32),
    ]
    mixed, field_modes = call(
        functools.partial(mix_kernel, own, rest, count, scale),
        "mix",
        3.9,
        there(1) + here(count + 1),
        [sent, sent],
        [pltpu.VMEM(modes[0], F32)] + mix_scratch,
    )(cot, mine, *arrived, weights)

    u_first = first_cells(field_modes, cell_count)
    ties = u_first[1:3]
    all_mixed = [mixed] + [send(mixed, "space", count, -k) for k in range(1, count)]
    plane_scratch = [pltpu.VMEM((count * own * height, 2 * LANES), BF16), pltpu.VMEM((rows, wide), BF16)]
    hidden, chan, mine, *others = call(
        functools.partial(middle_kernel, own, rest, count, planes, len(ties)),
        "middle",
        6.3,
        [pl.BlockSpec(memory_space=pltpu.SMEM)] + there(len(ties)) + here(count + 7),
        [((rows, columns), BF16), ((chans, LANES), F32), modes] + [tagged] * (count - 1),
        plane_scratch,
    )(place, *ties, *all_mixed, inverse, line, up_weight, flat, cot, local, basis)
    arrived = [send(array, "space", count, k + 1) for k, array in enumerate(others)]

    total, grad_modes = call(
        functools.partial(total_kernel, own, count), "total", 1.0, here(count + 1), [modes, tagged]
    )(mine, *arrived, chan)
    ties = u_first[3:]
    (returned,) = call(
        functools.partial(mix_back_kernel, own, rest, len(ties)),
        "mix_back",
        4.1,
        there(len(ties)) + here(2),
        [sent],
        mix_scratch + [pltpu.VMEM((2, 2 * chans * 8, LANES), F32)],
    )(*ties, total, weights)

    g_first = first_cells(grad_modes, cell_count)
    all_returned = [returned] + [send(returned, "space", count, -k) for k in range(1, count)]
    early_u, late_u = order_cells(field_modes, u_first, cell_count)
    early_g, late_g = order_cells(grad_modes, g_first, cell_count)
    sums = []
    if early_u:
        late_u = late_u + [swap(piece, 1, cell_count) for piece in late_u]
        ties = all_returned + g_first[3:] + late_u
        part, part_chan = early_gradient(early_u, early_g, ties, own, cell_norm)
        sums = [part, swap(part, 1, cell_count), part_chan, swap(part_chan, 1, cell_count)]
        late_g = late_g + [swap(piece, 1, cell_count) for piece in late_g]
    ties = sums[:1]
    (grad_fields,) = call(
        functools.partial(last_kernel, own, rest, count, block, len(ties)),
        "last",
        4.4,
        [pl.BlockSpec(memory_space=pltpu.SMEM)] + there(len(ties)) + here(count + 5),
        [(grid_like, BF16, pltpu.HBM)],
        plane_scratch
        + [
            pltpu.VMEM((ny_len, rows, nz_len), BF16),
            pltpu.VMEM(grid_like, BF16),
            pltpu.SemaphoreType.DMA((rows // block,)),
        ],
    )(place, *ties, *all_returned, inverse, down_weight, mix_down, hidden, basis)

    grad_spectral, grad_channel, grad_bias = weight_gradient(
        late_u, late_g, sums, spectral_weight.shape, (cell_norm, voxel_norm)
    )
    return (grad_fields.reshape(fields.shape), grad_spectral, grad_channel, grad_bias.reshape(chans))


def solution(mesh):
    in_specs = (
        P("dp", None, "space", None, None),
        P("dp", None, "space", None, None),
        P("space", None, None, None, None),
        P(),
        P(),
    )
    out_specs = (P("dp", None, "space", None, None), P("space", None, None, None, None), P(), P())
    body = functools.partial(shards, mesh.shape["space"], mesh.shape["dp"])
    return jax.shard_map(body, mesh=mesh, in_specs=in_specs, out_specs=out_specs, check_vma=False)
```
